128 devices in a mesh: row: 8 (over y, core), col: 4 (over x), layer: 4 (over z).
Axes of the slice: x: 4, y: 4, z: 4, core: 2. Of those that a mesh axis runs over, the one named last changes fastest.
Arguments:
- a_vals: bfloat16 [64, 16, 12, 128, 128], P('row', ('col', 'layer')), may hold values from -6 to 6
- a_cols: int32 [64, 16, 12], P('row', ('col', 'layer')), may hold values from 0 to 23, as said below
- b_vals: bfloat16 [384, 16, 128, 128], P(('col', 'layer'), 'row'), may hold values from -0.0546875 to 0.0546875
- b_cols: int32 [384, 16], P(('col', 'layer'), 'row'), may hold values from 0 to 31, as said below
- row_perm: int32 [64], replicated, may hold values from 0 to 63, as said below
Outputs:
- product: float32 [64, 32, 128, 128], P('row', ('col', 'layer'))
The draws below stay inside these ranges and needn't reach their ends.
Inputs may be any that keep to these rules, and one draw needn't show every extreme that they name: `a_cols`: within each left tile row and inner range the 12 entries are distinct. `b_cols`: within each right tile row the 16 entries are distinct. `row_perm`: a permutation; the 8 product rows of each index of row take exactly 1 left rows from each aligned block of 8 left rows.
All inputs are finite; a program needn't handle non-finite values.
Results may differ from the reference program's by a relative error of at most 0.0003.
Values may be sent and summed in bfloat16 or wider, within the bound.
A program may use at most 192 MiB of HBM per device.

```python
import jax
import jax.numpy as jnp
from jax import lax

TILE = 128
WR_DEV = 8
KA_R = 12
KWR = 24
KB = 16
NC = 32
WR = 64
RANGES = 16
KW = 384
N_ROW = 8


def pick_distinct(key, leading, choose, among):
    scores = jax.random.randint(key, leading + (among,), 0, 1 << 20, dtype=jnp.int32) * among
    scores = scores + jnp.arange(among, dtype=jnp.int32)
    return lax.top_k(scores, choose)[1].astype(jnp.int32)


def draw_a_cols(key, part):
    key = jax.random.fold_in(key, 21)
    return pick_distinct(key, (WR, RANGES), KA_R, KWR)


def draw_b_cols(key, part):
    key = jax.random.fold_in(key, 22)
    return pick_distinct(key, (KW,), KB, NC)


def draw_row_perm(key, part):
    key = jax.random.fold_in(key, 23)
    group = WR_DEV // N_ROW
    keys = jax.random.split(key, 2 * N_ROW)
    blocks = []
    for source in range(N_ROW):
        shuffled = jax.random.permutation(keys[source], WR_DEV).astype(jnp.int32) + source * WR_DEV
        blocks.append(shuffled.reshape(N_ROW, group))
    table = jnp.stack(blocks)
    result = []
    for target in range(N_ROW):
        incoming = table[:, target, :].reshape(WR_DEV)
        order = jax.random.permutation(keys[N_ROW + target], WR_DEV).astype(jnp.int32)
        result.append(jnp.take(incoming, order))
    return jnp.concatenate(result).astype(jnp.int32)


def levels(key, shape, cuts, low, top_value):
    loudness, own = 1.0, jax.random.fold_in(key, 6)
    for axis_at, parts in cuts:
        draws = jnp.exp(jax.random.uniform(jax.random.fold_in(own, axis_at), (parts,), jnp.float32, low / len(cuts), top_value / len(cuts)))
        loudness = loudness * jnp.repeat(draws, shape[axis_at] // parts).reshape([-1 if axis == axis_at else 1 for axis in range(len(shape))])
    return loudness


def scatter_about(stream_key, dims, spread, most, cuts=(), kind=jnp.bfloat16):
    entries = jax.random.normal(stream_key, dims, jnp.float32) * spread
    if len(cuts) > 0:
        entries = levels(stream_key, dims, cuts, -0.22, 0.18) * entries
    return jnp.clip(entries, min=-most, max=most).astype(kind)


def setup_inputs(seed: int = 0) -> dict:
    arg_keys = jax.random.split(jax.random.key(seed), 6)
    return {
        "a_vals": scatter_about(arg_keys[0], (WR, RANGES, KA_R, TILE, TILE), 1.0, 6.0, ((0, 8), (1, 16))),
        "a_cols": draw_a_cols(jax.random.fold_in(arg_keys[5], 71), 0),
        "b_vals": scatter_about(arg_keys[2], (KW, KB, TILE, TILE), (TILE * RANGES * KA_R * KB // NC) ** -0.5, 0.0546875, ((0, 16), (1, 8))),
        "b_cols": draw_b_cols(jax.random.fold_in(arg_keys[5], 71), 0),
        "row_perm": draw_row_perm(jax.random.fold_in(arg_keys[5], 71), 0),
    }


def reference(a_vals, a_cols, b_vals, b_cols, row_perm):
    left_vals = jnp.take(a_vals, row_perm, axis=0)
    left_cols = jnp.take(a_cols, row_perm, axis=0)

    def add_range(g, total):
        index = jnp.asarray(g).astype(jnp.int32)
        start = index * KWR
        block = lax.dynamic_slice_in_dim(b_vals, start, KWR, 0)
        block_cols = lax.dynamic_slice_in_dim(b_cols, start, KWR, 0)
        vals_g = lax.dynamic_index_in_dim(left_vals, index, 1, keepdims=False)
        cols_g = lax.dynamic_index_in_dim(left_cols, index, 1, keepdims=False)

        def one_row(pair):
            vals, cols = pair
            picked = jnp.take(block, cols, axis=0)
            targets = jnp.take(block_cols, cols, axis=0).reshape(-1)
            prods = jnp.einsum("kab,kmbc->kmac", vals.astype(jnp.float32), picked.astype(jnp.float32))
            prods = prods.reshape(KA_R * KB, TILE, TILE)
            return jnp.zeros((NC, TILE, TILE), jnp.float32).at[targets].add(prods)

        return total + lax.map(one_row, (vals_g, cols_g))

    start_total = jnp.zeros((WR, NC, TILE, TILE), jnp.float32)
    return lax.fori_loop(0, RANGES, add_range, start_total)
```

```python
import functools

import jax
import jax.numpy as jnp
from jax import lax
from jax.experimental import pallas as pl
from jax.experimental.pallas import tpu as pltpu
from jax.sharding import PartitionSpec as P

TILE = 128
NC = 32
KWR = 24
KA = 12
ROWS = 8
RING = 4
CHUNK = 4
NCH = KWR // CHUNK
PIECE = CHUNK * 2
HALF = PIECE // 2
NB = 256
TOP = 32767.0
PHASES = (2, 1, 3, 0)
MESH = pl.DeviceIdType.MESH


def encode(v):
    top = jnp.maximum(jnp.max(jnp.abs(v), axis=0, keepdims=True), 1e-30)
    coded = jnp.round(v * (TOP / top)).astype(jnp.int32).astype(jnp.int16)
    return coded, top * (1.0 / TOP)


def decode(coded, scale):
    return coded.astype(jnp.int32).astype(jnp.float32) * scale


def kernel(
    ia, ib, a_hbm, b_hbm, out,
    a_v, b_v0, b_v1, b_v2, b_v3, b_v4, b_v5, ad, bd, acc,
    s1, s1s, r1, r1s, s2, s2s, r2, r2s, s3, s3s, r3, r3s, fin,
    g_send, g_recv, loc_sem, m_send, m_recv, y_send, y_recv,
):
    b_v = (b_v0, b_v1, b_v2, b_v3, b_v4, b_v5)
    row = lax.axis_index("row")
    x = lax.axis_index("col")
    z = lax.axis_index("layer")
    y, c = row // 2, lax.rem(row, 2)

    def at_row(dy, dc):
        return lax.rem(y + dy, RING) * 2 + lax.rem(c + dc, 2)

    def dev_row(dy, dc):
        return (at_row(dy, dc), x, z)

    def dev_f(h, df):
        if h == 0:
            return (row, lax.rem(x + df, RING), z)
        return (row, x, lax.rem(z + df, RING))

    barrier = pltpu.get_barrier_semaphore()
    peers = [dev_row(dy, dc) for dy in range(RING) for dc in range(2) if dy or dc]
    peers += [dev_f(h, df) for h in range(2) for df in range(1, RING)]
    for peer in peers:
        pl.semaphore_signal(barrier, inc=1, device_id=peer, device_id_type=MESH)

    a_copy = pltpu.make_async_copy(a_hbm, a_v.at[pl.ds(0, ROWS * KA)], loc_sem.at[NCH])
    a_copy.start()
    own = [
        pltpu.make_async_copy(
            b_hbm.at[pl.ds(q * PIECE, PIECE)], b_v[q].at[pl.ds(row * PIECE, PIECE)], loc_sem.at[q]
        )
        for q in range(NCH)
    ]
    for q in range(NCH):
        own[q].start()
    zero = jnp.zeros((TILE, TILE), jnp.bfloat16)
    a_v[ROWS * KA] = zero
    for q in range(NCH):
        b_v[q][ROWS * PIECE] = zero
    pl.semaphore_wait(barrier, len(peers))

    def g_copy(q, kind, src, dst_at, n, target):
        return pltpu.make_async_remote_copy(
            src_ref=src,
            dst_ref=b_v[q].at[pl.ds(dst_at, n)],
            send_sem=g_send.at[q, kind],
            recv_sem=g_recv.at[q, kind],
            device_id=target,
            device_id_type=MESH,
        )

    up, down, sib = dev_row(1, 0), dev_row(3, 0), dev_row(0, 1)
    at_own, at_below, at_above, at_far = (at_row(d, 0) * PIECE for d in (0, 3, 1, 2))

    def g_all(q):
        mine = b_hbm.at[pl.ds(q * PIECE, PIECE)]
        held = lambda at, n: b_v[q].at[pl.ds(at, n)]
        return (
            g_copy(q, 0, mine, at_own, PIECE, up),
            g_copy(q, 1, mine, at_own, PIECE, down),
            g_copy(q, 2, mine, at_own, PIECE, sib),
            g_copy(q, 3, held(at_below, HALF), at_below, HALF, up),
            g_copy(q, 4, held(at_above + HALF, HALF), at_above + HALF, HALF, down),
            g_copy(q, 5, held(at_below, PIECE), at_below, PIECE, sib),
            g_copy(q, 6, held(at_above, PIECE), at_above, PIECE, sib),
            g_copy(q, 7, held(at_far, HALF), at_far, HALF, sib),
            g_copy(q, 8, held(at_far + HALF, HALF), at_far + HALF, HALF, sib),
        )

    copies = [g_all(q) for q in range(NCH)]

    def first(q):
        for kind in (0, 1, 2):
            copies[q][kind].start()

    def relay(q):
        copies[q][0].wait_recv()
        copies[q][3].start()
        copies[q][5].start()
        copies[q][1].wait_recv()
        copies[q][4].start()
        copies[q][6].start()

    def pass_on(q):
        copies[q][3].wait_recv()
        copies[q][7].start()
        copies[q][4].wait_recv()
        copies[q][8].start()

    def arrived(q):
        own[q].wait()
        for kind in (2, 5, 6, 7, 8):
            copies[q][kind].wait_recv()

    def dense_a(q):
        for t, dy in enumerate(PHASES):
            for h in range(2):
                d = 2 * t + h
                base = at_row(dy, h) * KWR + q * CHUNK
                for k in range(CHUNK):
                    ad[d * TILE : (d + 1) * TILE, k * TILE : (k + 1) * TILE] = a_v[ia[base + k]]

    def dense_b(q):
        for k in range(CHUNK):

            @pl.loop(0, NC, unroll=8)
            def _(col):
                at = pl.multiple_of(col * TILE, TILE)
                bd[k * TILE : (k + 1) * TILE, pl.ds(at, TILE)] = b_v[q][
                    ib[(q * CHUNK + k) * NC + col]
                ]

    def multiply(r0, r1_, n0, n1, begin):
        @pl.loop(n0, n1)
        def _(n):
            cols = pl.ds(pl.multiple_of(n * NB, NB), NB)
            part = jnp.dot(ad[r0:r1_, :], bd[:, cols], preferred_element_type=jnp.float32)
            if begin:
                acc[r0:r1_, cols] = part
            else:
                acc[r0:r1_, cols] = acc[r0:r1_, cols] + part

    def pos(h):
        return (x, z) if h == 0 else (z, x)

    def block(h, f_at, s_at):
        return f_at * RING + s_at if h == 0 else s_at * RING + f_at

    def held_tile(d, h, f_at, s_at, cc):
        lanes = pl.ds(pl.multiple_of(block(h, f_at, s_at) * 2 * TILE + cc * TILE, TILE), TILE)
        return (slice(d * TILE, (d + 1) * TILE), lanes)

    def m_copy(d, kind, src, dst, target):
        return pltpu.make_async_remote_copy(
            src_ref=src,
            dst_ref=dst,
            send_sem=m_send.at[d, kind],
            recv_sem=m_recv.at[d, kind],
            device_id=target,
            device_id_type=MESH,
        )

    def m_all(d, h):
        res = []
        for way in range(2):
            target = dev_f(h, 1 if way == 0 else 3)
            res.append(m_copy(d, 2 * way, s1.at[d, way], r1.at[d, way], target))
            res.append(m_copy(d, 2 * way + 1, s1s.at[d, way], r1s.at[d, way], target))
        for way in range(2):
            target = dev_f(h, 1 if way == 0 else 3)
            res.append(m_copy(d, 4 + 2 * way, s2.at[d, way], r2.at[d, way], target))
            res.append(m_copy(d, 5 + 2 * way, s2s.at[d, way], r2s.at[d, way], target))
        for ds in range(1, RING):
            target = dev_f(1 - h, ds)
            res.append(m_copy(d, 6 + 2 * ds, s3.at[d, ds - 1], r3.at[d, ds - 1], target))
            res.append(m_copy(d, 7 + 2 * ds, s3s.at[d, ds - 1], r3s.at[d, ds - 1], target))
        return res

    m = [m_all(d, d % 2) for d in range(ROWS)]

    def far_part(d):
        h = d % 2
        f, _ = pos(h)
        f2 = lax.rem(f + 2, RING)
        for way in range(2):

            @pl.loop(0, 4)
            def _(i):
                v = acc[held_tile(d, h, f2, way * 2 + i // 2, lax.rem(i, 2))]
                coded, scale = encode(v)
                s1[d, way, i] = coded
                s1s[d, way, pl.ds(i, 1), :] = scale

            m[d][2 * way].start()
            m[d][2 * way + 1].start()

    def near_part(d):
        h = d % 2
        f, _ = pos(h)
        for way in range(2):
            fd = lax.rem(f + (1 if way == 0 else 3), RING)
            m[d][2 * way].wait_recv()
            m[d][2 * way + 1].wait_recv()

            @pl.loop(0, 4)
            def _(i):
                v = acc[held_tile(d, h, fd, (1 - way) * 2 + i // 2, lax.rem(i, 2))]
                coded, scale = encode(v)
                s2[d, way, (1 - way) * 4 + i] = coded
                s2s[d, way, pl.ds((1 - way) * 4 + i, 1), :] = scale

            @pl.loop(0, 4)
            def _(i):
                v = acc[held_tile(d, h, fd, way * 2 + i // 2, lax.rem(i, 2))]
                v = v + decode(r1[d, way, i], r1s[d, way, pl.ds(i, 1), :])
                coded, scale = encode(v)
                s2[d, way, way * 4 + i] = coded
                s2s[d, way, pl.ds(way * 4 + i, 1), :] = scale

            m[d][4 + 2 * way].start()
            m[d][5 + 2 * way].start()

    def second(d):
        h = d % 2
        f, s = pos(h)
        for kind in range(4, 8):
            m[d][kind].wait_recv()
        for ds in (1, 2, 3, 0):
            s_at = lax.rem(s + ds, RING)

            @pl.loop(0, 2)
            def _(cc):
                where = held_tile(d, h, f, s_at, cc)
                i = s_at * 2 + cc
                v = (
                    acc[where]
                    + decode(r2[d, 0, i], r2s[d, 0, pl.ds(i, 1), :])
                    + decode(r2[d, 1, i], r2s[d, 1, pl.ds(i, 1), :])
                )
                if ds == 0:
                    fin[d, cc] = v
                else:
                    coded, scale = encode(v)
                    s3[d, ds - 1, cc] = coded
                    s3s[d, ds - 1, pl.ds(cc, 1), :] = scale

            if ds:
                m[d][6 + 2 * ds].start()
                m[d][7 + 2 * ds].start()

    y_copies = []
    for t, dy in enumerate(PHASES):
        for h in range(2):
            d = 2 * t + h
            if dy or h:
                y_copies.append(
                    pltpu.make_async_remote_copy(
                        src_ref=fin.at[d],
                        dst_ref=out.at[row],
                        send_sem=y_send.at[d],
                        recv_sem=y_recv.at[d],
                        device_id=dev_row(dy, h),
                        device_id_type=MESH,
                    )
                )
            else:
                y_copies.append(pltpu.make_async_copy(fin.at[d], out.at[row], y_send.at[d]))

    def last(d):
        for kind in range(8, 14):
            m[d][kind].wait_recv()

        @pl.loop(0, 2)
        def _(cc):
            v = fin[d, cc]
            for k in range(3):
                v = v + decode(r3[d, k, cc], r3s[d, k, pl.ds(cc, 1), :])
            fin[d, cc] = v

        y_copies[d].start()

    def both(step, t):
        step(2 * t)
        step(2 * t + 1)

    first(0)
    first(1)
    first(2)
    relay(0)
    pass_on(0)
    a_copy.wait()
    arrived(0)
    nsteps = NC * TILE // NB
    for q in range(NCH - 1):
        relay(q + 1)
        if q + 3 < NCH:
            first(q + 3)
        dense_a(q)
        dense_b(q)
        multiply(0, ROWS * TILE, 0, nsteps // 2, q == 0)
        pass_on(q + 1)
        multiply(0, ROWS * TILE, nsteps // 2, nsteps, q == 0)
        arrived(q + 1)
    dense_a(NCH - 1)
    dense_b(NCH - 1)

    def ready(t):
        multiply(2 * t * TILE, 2 * (t + 1) * TILE, 0, nsteps, False)
        both(far_part, t)

    ready(0)
    ready(1)
    both(near_part, 0)
    ready(2)
    both(near_part, 1)
    both(second, 0)
    ready(3)
    both(near_part, 2)
    both(second, 1)
    both(last, 0)
    both(near_part, 3)
    both(second, 2)
    both(last, 1)
    both(second, 3)
    both(last, 2)
    both(last, 3)

    for q in range(NCH):
        for copy in copies[q]:
            copy.wait_send()
    for d in range(ROWS):
        for copy in m[d]:
            copy.wait_send()
        t, h = d // 2, d % 2
        if PHASES[t] or h:
            y_copies[d].wait()
        else:
            y_copies[d].wait()


def exchange(ia, ib, a_vals, b_vals):
    bf16, f32, i16 = jnp.bfloat16, jnp.float32, jnp.int16
    t2 = (TILE, TILE)
    b_chunk = pltpu.VMEM((ROWS * PIECE + 1, *t2), bf16)
    dma = pltpu.SemaphoreType.DMA
    return pl.pallas_call(
        kernel,
        out_shape=jax.ShapeDtypeStruct((ROWS, 2, *t2), f32),
        in_specs=[
            pl.BlockSpec(memory_space=pltpu.SMEM),
            pl.BlockSpec(memory_space=pltpu.SMEM),
            pl.BlockSpec(memory_space=pl.ANY),
            pl.BlockSpec(memory_space=pl.ANY),
        ],
        out_specs=pl.BlockSpec(memory_space=pl.ANY),
        scratch_shapes=[
            pltpu.VMEM((ROWS * KA + 1, *t2), bf16),
            b_chunk, b_chunk, b_chunk, b_chunk, b_chunk, b_chunk,
            pltpu.VMEM((ROWS * TILE, CHUNK * TILE), bf16),
            pltpu.VMEM((CHUNK * TILE, NC * TILE), bf16),
            pltpu.VMEM((ROWS * TILE, NC * TILE), f32),
            pltpu.VMEM((ROWS, 2, 4, *t2), i16),
            pltpu.VMEM((ROWS, 2, 8, TILE), f32),
            pltpu.VMEM((ROWS, 2, 4, *t2), i16),
            pltpu.VMEM((ROWS, 2, 8, TILE), f32),
            pltpu.VMEM((ROWS, 2, 8, *t2), i16),
            pltpu.VMEM((ROWS, 2, 8, TILE), f32),
            pltpu.VMEM((ROWS, 2, 8, *t2), i16),
            pltpu.VMEM((ROWS, 2, 8, TILE), f32),
            pltpu.VMEM((ROWS, 3, 2, *t2), i16),
            pltpu.VMEM((ROWS, 3, 8, TILE), f32),
            pltpu.VMEM((ROWS, 3, 2, *t2), i16),
            pltpu.VMEM((ROWS, 3, 8, TILE), f32),
            pltpu.VMEM((ROWS, 2, *t2), f32),
            dma((NCH, 9)), dma((NCH, 9)), dma((NCH + 1,)),
            dma((ROWS, 14)), dma((ROWS, 14)), dma((ROWS,)), dma((ROWS,)),
        ],
        compiler_params=pltpu.CompilerParams(
            collective_id=0, has_side_effects=True, vmem_limit_bytes=60 * 1024 * 1024
        ),
        name="exchange",
    )(ia, ib, a_vals, b_vals)


def on_device(a_vals, a_cols, b_vals, b_cols, row_perm):
    own_row = lax.axis_index("row")
    i32 = jnp.int32
    perm = row_perm.reshape(ROWS, ROWS)
    taken = jnp.sum(jnp.where(perm // ROWS == own_row, perm % ROWS, 0), axis=1)
    hot_row = taken[:, None] == jnp.arange(ROWS, dtype=i32)[None, :]
    cols = jnp.sum(jnp.where(hot_row[:, :, None], a_cols[:, 0][None], 0), axis=1)
    hot = cols[:, :, None] == jnp.arange(KWR, dtype=i32)
    at = taken[:, None] * KA + jnp.arange(KA, dtype=i32)[None, :]
    none = ROWS * KA
    ia = none + jnp.sum(jnp.where(hot, at[:, :, None] - none, 0), axis=1)
    bc = lax.all_gather(b_cols, "row", axis=1, tiled=True)
    slot = jnp.arange(2 * ROWS, dtype=i32)[None, :]
    r = jnp.arange(KWR, dtype=i32)[:, None]
    at = slot // 2 * PIECE + r % CHUNK * 2 + slot % 2
    none = ROWS * PIECE
    hot = bc[:, :, None] == jnp.arange(NC, dtype=i32)
    ib = none + jnp.sum(jnp.where(hot, at[:, :, None] - none, 0), axis=1)
    got = exchange(
        ia.reshape(-1),
        ib.reshape(-1),
        a_vals.reshape(ROWS * KA, TILE, TILE),
        b_vals.reshape(KWR * 2, TILE, TILE),
    )
    source = lax.dynamic_slice_in_dim(row_perm, own_row * ROWS, ROWS) // ROWS
    return jnp.take(got, source, axis=0)


def solution(mesh):
    placed = (
        P("row", ("col", "layer"), None, None, None),
        P("row", ("col", "layer"), None),
        P(("col", "layer"), "row", None, None),
        P(("col", "layer"), "row"),
        P(),
    )
    return jax.shard_map(
        on_device,
        mesh=mesh,
        in_specs=placed,
        out_specs=P("row", ("col", "layer"), None, None),
        check_vma=False,
    )
```

```python
import functools

import jax
import jax.numpy as jnp
from jax import lax
from jax.experimental import pallas as pl
from jax.experimental.pallas import tpu as pltpu
from jax.sharding import PartitionSpec as P

TILE = 128
NC = 32
KWR = 24
KA = 12
ROWS = 8
RING = 4
CHUNK = 4
NCH = KWR // CHUNK
PIECE = CHUNK * 2
HALF = PIECE // 2
NB = 1024
NSTEP = NC * TILE // NB
TOP = 32767.0
UNROLL = 4
PHASES = (2, 1, 3, 0)
MESH = pl.DeviceIdType.MESH


def encode(v):
    top = jnp.maximum(jnp.max(jnp.abs(v), axis=0, keepdims=True), 1e-30)
    coded = jnp.round(v * (TOP / top)).astype(jnp.int32).astype(jnp.int16)
    return coded, top * (1.0 / TOP)


def decode(coded, scale):
    return coded.astype(jnp.int32).astype(jnp.float32) * scale


def kernel(
    perm, ac_ref, bc_ref, a_hbm, b_hbm, out,
    a_v, b_v0, b_v1, b_v2, b_v3, b_v4, b_v5, ad, acc, ia_v, bc_v, ib_v, w_own, w_all, ia, ib,
    s1, s1s, r1, r1s, s2, s2s, r2, r2s, s3, s3s, r3, r3s, fin,
    g_send, g_recv, loc_sem, w_send, w_recv, m_send, m_recv, y_send, y_recv,
):
    b_v = (b_v0, b_v1, b_v2, b_v3, b_v4, b_v5)
    row = lax.axis_index("row")
    x = lax.axis_index("col")
    z = lax.axis_index("layer")
    y, c = row // 2, lax.rem(row, 2)

    def at_row(dy, dc):
        return lax.rem(y + dy, RING) * 2 + lax.rem(c + dc, 2)

    def dev_row(dy, dc):
        return (at_row(dy, dc), x, z)

    def dev_f(h, df):
        if h == 0:
            return (row, lax.rem(x + df, RING), z)
        return (row, x, lax.rem(z + df, RING))

    barrier = pltpu.get_barrier_semaphore()
    peers = [dev_row(dy, dc) for dy in range(RING) for dc in range(2) if dy or dc]
    peers += [dev_f(h, df) for h in range(2) for df in range(1, RING)]
    for peer in peers:
        pl.semaphore_signal(barrier, inc=1, device_id=peer, device_id_type=MESH)

    lane = lax.broadcasted_iota(jnp.int32, (ROWS, TILE), 1)
    left = lax.broadcasted_iota(jnp.int32, (ROWS, TILE), 0)
    table = jnp.full((ROWS, TILE), ROWS * KA, jnp.int32)
    for k in range(KA):
        table = jnp.where(ac_ref[:, k : k + 1] == lane, left * KA + k, table)
    ia_v[...] = table
    ia_copy = pltpu.make_async_copy(ia_v, ia, loc_sem.at[NCH + 1])
    ia_copy.start()
    bc_v[...] = jnp.full((ROWS, TILE), -1, jnp.int32)
    bc_v[0:2, 0:KWR] = bc_ref[...]
    col = lax.broadcasted_iota(jnp.int32, (NC, TILE), 0)
    inner = lax.rem(lax.broadcasted_iota(jnp.int32, (NC, TILE), 1), CHUNK)
    table = jnp.zeros((NC, TILE), jnp.int32)
    for k in range(2):
        table = jnp.where(bc_v[k : k + 1, :] == col, row * PIECE + inner * 2 + k + 1, table)
    w_own[...] = table

    a_copy = pltpu.make_async_copy(a_hbm, a_v.at[pl.ds(0, ROWS * KA)], loc_sem.at[NCH])
    a_copy.start()
    own = [
        pltpu.make_async_copy(
            b_hbm.at[pl.ds(q * PIECE, PIECE)], b_v[q].at[pl.ds(row * PIECE, PIECE)], loc_sem.at[q]
        )
        for q in range(NCH)
    ]
    for q in range(NCH):
        own[q].start()
    zero = jnp.zeros((TILE, TILE), jnp.bfloat16)
    a_v[ROWS * KA] = zero
    for q in range(NCH):
        b_v[q][ROWS * PIECE] = zero
    pl.semaphore_wait(barrier, len(peers))

    w_copies = [
        pltpu.make_async_remote_copy(
            src_ref=w_own,
            dst_ref=w_all.at[row],
            send_sem=w_send.at[2 * dy + dc],
            recv_sem=w_recv.at[2 * dy + dc],
            device_id=dev_row(dy, dc),
            device_id_type=MESH,
        )
        for dy in range(RING)
        for dc in range(2)
        if dy or dc
    ]
    for copy in w_copies:
        copy.start()

    def tables():
        w_all[row] = w_own[...]
        for copy in w_copies:
            copy.wait_recv()
        top = w_all[0]
        for source in range(1, ROWS):
            top = jnp.maximum(top, w_all[source])
        ib_v[...] = jnp.where(top > 0, top - 1, ROWS * PIECE)
        ib_copy = pltpu.make_async_copy(ib_v, ib, loc_sem.at[NCH + 2])
        ib_copy.start()
        ib_copy.wait()
        ia_copy.wait()

    def g_copy(q, kind, src, dst_at, n, target):
        return pltpu.make_async_remote_copy(
            src_ref=src,
            dst_ref=b_v[q].at[pl.ds(dst_at, n)],
            send_sem=g_send.at[q, kind],
            recv_sem=g_recv.at[q, kind],
            device_id=target,
            device_id_type=MESH,
        )

    up, down, sib = dev_row(1, 0), dev_row(3, 0), dev_row(0, 1)
    at_own, at_below, at_above, at_far = (at_row(d, 0) * PIECE for d in (0, 3, 1, 2))

    def g_all(q):
        mine = b_hbm.at[pl.ds(q * PIECE, PIECE)]
        held = lambda at, n: b_v[q].at[pl.ds(at, n)]
        return (
            g_copy(q, 0, mine, at_own, PIECE, up),
            g_copy(q, 1, mine, at_own, PIECE, down),
            g_copy(q, 2, mine, at_own, PIECE, sib),
            g_copy(q, 3, held(at_below, HALF), at_below, HALF, up),
            g_copy(q, 4, held(at_above + HALF, HALF), at_above + HALF, HALF, down),
            g_copy(q, 5, held(at_below, PIECE), at_below, PIECE, sib),
            g_copy(q, 6, held(at_above, PIECE), at_above, PIECE, sib),
            g_copy(q, 7, held(at_far, HALF), at_far, HALF, sib),
            g_copy(q, 8, held(at_far + HALF, HALF), at_far + HALF, HALF, sib),
        )

    copies = [g_all(q) for q in range(NCH)]

    def first(q):
        for kind in (0, 1, 2):
            copies[q][kind].start()

    def relay(q):
        copies[q][0].wait_recv()
        copies[q][3].start()
        copies[q][5].start()
        copies[q][1].wait_recv()
        copies[q][4].start()
        copies[q][6].start()

    def pass_on(q):
        copies[q][3].wait_recv()
        copies[q][7].start()
        copies[q][4].wait_recv()
        copies[q][8].start()

    def arrived(q):
        own[q].wait()
        for kind in (2, 5, 6, 7, 8):
            copies[q][kind].wait_recv()

    def taken(j):
        total = jnp.int32(0)
        for i in range(ROWS):
            p = perm[j * ROWS + i]
            total = jnp.maximum(total, jnp.where(lax.div(p, ROWS) == row, lax.rem(p, ROWS), 0))
        return total

    def dense_a(q, rows):
        for d in range(ROWS):
            for k in range(CHUNK):
                ad[d * TILE : (d + 1) * TILE, k * TILE : (k + 1) * TILE] = a_v[
                    ia[rows[d], q * CHUNK + k]
                ]

    def multiply(q, r0, r1_, hooks=()):
        @pl.loop(0, NSTEP)
        def _(n):
            for step, act in hooks:
                pl.when(n == step)(act)
            wide = NB // TILE
            right = jnp.concatenate(
                [
                    jnp.concatenate(
                        [b_v[q][ib[n * wide + i, q * CHUNK + k]] for i in range(wide)], axis=1
                    )
                    for k in range(CHUNK)
                ],
                axis=0,
            )
            cols = pl.ds(pl.multiple_of(n * NB, NB), NB)
            part = jnp.dot(ad[r0:r1_, :], right, preferred_element_type=jnp.float32)
            if q == 0:
                acc[r0:r1_, cols] = part
            else:
                acc[r0:r1_, cols] = acc[r0:r1_, cols] + part

    def pos(h):
        return (x, z) if h == 0 else (z, x)

    def block(h, f_at, s_at):
        return f_at * RING + s_at if h == 0 else s_at * RING + f_at

    def held_tile(d, h, f_at, s_at, cc):
        lanes = pl.ds(pl.multiple_of(block(h, f_at, s_at) * 2 * TILE + cc * TILE, TILE), TILE)
        return (slice(d * TILE, (d + 1) * TILE), lanes)

    def m_copy(d, kind, src, dst, target):
        return pltpu.make_async_remote_copy(
            src_ref=src,
            dst_ref=dst,
            send_sem=m_send.at[d, kind],
            recv_sem=m_recv.at[d, kind],
            device_id=target,
            device_id_type=MESH,
        )

    def m_all(d, h):
        res = []
        for way in range(2):
            target = dev_f(h, 1 if way == 0 else 3)
            res.append(m_copy(d, 2 * way, s1.at[d, way], r1.at[d, way], target))
            res.append(m_copy(d, 2 * way + 1, s1s.at[d, way], r1s.at[d, way], target))
        for way in range(2):
            target = dev_f(h, 1 if way == 0 else 3)
            res.append(m_copy(d, 4 + 2 * way, s2.at[d, way], r2.at[d, way], target))
            res.append(m_copy(d, 5 + 2 * way, s2s.at[d, way], r2s.at[d, way], target))
        for ds in range(1, RING):
            target = dev_f(1 - h, ds)
            res.append(m_copy(d, 6 + 2 * ds, s3.at[d, ds - 1], r3.at[d, ds - 1], target))
            res.append(m_copy(d, 7 + 2 * ds, s3s.at[d, ds - 1], r3s.at[d, ds - 1], target))
        return res

    m = [m_all(d, d % 2) for d in range(ROWS)]

    def far_part(d):
        h = d % 2
        f, _ = pos(h)
        f2 = lax.rem(f + 2, RING)
        for way in range(2):

            @pl.loop(0, 4, unroll=UNROLL)
            def _(i):
                v = acc[held_tile(d, h, f2, way * 2 + i // 2, lax.rem(i, 2))]
                coded, scale = encode(v)
                s1[d, way, i] = coded
                s1s[d, way, pl.ds(i, 1), :] = scale

            m[d][2 * way].start()
            m[d][2 * way + 1].start()

    def near_part(d):
        h = d % 2
        f, _ = pos(h)
        for way in range(2):
            fd = lax.rem(f + (1 if way == 0 else 3), RING)
            m[d][2 * way].wait_recv()
            m[d][2 * way + 1].wait_recv()

            @pl.loop(0, 4, unroll=UNROLL)
            def _(i):
                v = acc[held_tile(d, h, fd, (1 - way) * 2 + i // 2, lax.rem(i, 2))]
                coded, scale = encode(v)
                s2[d, way, (1 - way) * 4 + i] = coded
                s2s[d, way, pl.ds((1 - way) * 4 + i, 1), :] = scale

            @pl.loop(0, 4, unroll=UNROLL)
            def _(i):
                v = acc[held_tile(d, h, fd, way * 2 + i // 2, lax.rem(i, 2))]
                v = v + decode(r1[d, way, i], r1s[d, way, pl.ds(i, 1), :])
                coded, scale = encode(v)
                s2[d, way, way * 4 + i] = coded
                s2s[d, way, pl.ds(way * 4 + i, 1), :] = scale

            m[d][4 + 2 * way].start()
            m[d][5 + 2 * way].start()

    def second(d):
        h = d % 2
        f, s = pos(h)
        for kind in range(4, 8):
            m[d][kind].wait_recv()
        for ds in (1, 2, 3, 0):
            s_at = lax.rem(s + ds, RING)

            @pl.loop(0, 2, unroll=2)
            def _(cc):
                where = held_tile(d, h, f, s_at, cc)
                i = s_at * 2 + cc
                v = (
                    acc[where]
                    + decode(r2[d, 0, i], r2s[d, 0, pl.ds(i, 1), :])
                    + decode(r2[d, 1, i], r2s[d, 1, pl.ds(i, 1), :])
                )
                if ds == 0:
                    fin[d, cc] = v
                else:
                    coded, scale = encode(v)
                    s3[d, ds - 1, cc] = coded
                    s3s[d, ds - 1, pl.ds(cc, 1), :] = scale

            if ds:
                m[d][6 + 2 * ds].start()
                m[d][7 + 2 * ds].start()

    y_copies = []
    for t, dy in enumerate(PHASES):
        for h in range(2):
            d = 2 * t + h
            if dy or h:
                y_copies.append(
                    pltpu.make_async_remote_copy(
                        src_ref=fin.at[d],
                        dst_ref=out.at[row],
                        send_sem=y_send.at[d],
                        recv_sem=y_recv.at[d],
                        device_id=dev_row(dy, h),
                        device_id_type=MESH,
                    )
                )
            else:
                y_copies.append(pltpu.make_async_copy(fin.at[d], out.at[row], y_send.at[d]))

    def last(d):
        for kind in range(8, 14):
            m[d][kind].wait_recv()

        @pl.loop(0, 2, unroll=2)
        def _(cc):
            v = fin[d, cc]
            for k in range(3):
                v = v + decode(r3[d, k, cc], r3s[d, k, pl.ds(cc, 1), :])
            fin[d, cc] = v

        y_copies[d].start()

    def both(step, t):
        step(2 * t)
        step(2 * t + 1)

    first(0)
    first(1)
    tables()
    rows = [taken(at_row(dy, h)) for dy in PHASES for h in range(2)]
    relay(0)
    first(2)
    relay(1)
    first(3)
    pass_on(0)
    a_copy.wait()
    arrived(0)
    for q in range(NCH - 1):
        dense_a(q, rows)
        hooks = []
        if q + 2 < NCH:

            def onward(q=q):
                relay(q + 2)
                if q + 4 < NCH:
                    first(q + 4)

            hooks.append((NSTEP - 1, onward))
        else:
            hooks.append((NSTEP - 2, functools.partial(pass_on, q + 1)))
        multiply(q, 0, ROWS * TILE, hooks)
        if q + 2 < NCH:
            pass_on(q + 1)
        arrived(q + 1)
    dense_a(NCH - 1, rows)

    def ready(t):
        multiply(NCH - 1, 2 * t * TILE, 2 * (t + 1) * TILE)
        both(far_part, t)

    ready(0)
    ready(1)
    both(near_part, 0)
    ready(2)
    both(near_part, 1)
    ready(3)
    both(near_part, 2)
    both(second, 0)
    both(near_part, 3)
    both(second, 1)
    both(last, 0)
    both(second, 2)
    both(last, 1)
    both(second, 3)
    both(last, 2)
    both(last, 3)

    for copy in w_copies:
        copy.wait_send()
    for q in range(NCH):
        for copy in copies[q]:
            copy.wait_send()
    for d in range(ROWS):
        for copy in m[d]:
            copy.wait_send()
        y_copies[d].wait()


def exchange(row_perm, a_cols, b_cols, a_vals, b_vals):
    bf16, f32, i16, i32 = jnp.bfloat16, jnp.float32, jnp.int16, jnp.int32
    t2 = (TILE, TILE)
    b_chunk = pltpu.VMEM((ROWS * PIECE + 1, *t2), bf16)
    dma = pltpu.SemaphoreType.DMA
    return pl.pallas_call(
        kernel,
        out_shape=jax.ShapeDtypeStruct((ROWS, 2, *t2), f32),
        in_specs=[
            pl.BlockSpec(memory_space=pltpu.SMEM),
            pl.BlockSpec(memory_space=pltpu.VMEM),
            pl.BlockSpec(memory_space=pltpu.VMEM),
            pl.BlockSpec(memory_space=pl.ANY),
            pl.BlockSpec(memory_space=pl.ANY),
        ],
        out_specs=pl.BlockSpec(memory_space=pl.ANY),
        scratch_shapes=[
            pltpu.VMEM((ROWS * KA + 1, *t2), bf16),
            b_chunk, b_chunk, b_chunk, b_chunk, b_chunk, b_chunk,
            pltpu.VMEM((ROWS * TILE, CHUNK * TILE), bf16),
            pltpu.VMEM((ROWS * TILE, NC * TILE), f32),
            pltpu.VMEM((ROWS, TILE), i32),
            pltpu.VMEM((ROWS, TILE), i32),
            pltpu.VMEM((NC, TILE), i32),
            pltpu.VMEM((NC, TILE), i32),
            pltpu.VMEM((ROWS, NC, TILE), i32),
            pltpu.SMEM((ROWS, TILE), i32),
            pltpu.SMEM((NC, TILE), i32),
            pltpu.VMEM((ROWS, 2, 4, *t2), i16),
            pltpu.VMEM((ROWS, 2, 8, TILE), f32),
            pltpu.VMEM((ROWS, 2, 4, *t2), i16),
            pltpu.VMEM((ROWS, 2, 8, TILE), f32),
            pltpu.VMEM((ROWS, 2, 8, *t2), i16),
            pltpu.VMEM((ROWS, 2, 8, TILE), f32),
            pltpu.VMEM((ROWS, 2, 8, *t2), i16),
            pltpu.VMEM((ROWS, 2, 8, TILE), f32),
            pltpu.VMEM((ROWS, 3, 2, *t2), i16),
            pltpu.VMEM((ROWS, 3, 8, TILE), f32),
            pltpu.VMEM((ROWS, 3, 2, *t2), i16),
            pltpu.VMEM((ROWS, 3, 8, TILE), f32),
            pltpu.VMEM((ROWS, 2, *t2), f32),
            dma((NCH, 9)), dma((NCH, 9)), dma((NCH + 3,)), dma((ROWS,)), dma((ROWS,)),
            dma((ROWS, 14)), dma((ROWS, 14)), dma((ROWS,)), dma((ROWS,)),
        ],
        compiler_params=pltpu.CompilerParams(
            collective_id=0, has_side_effects=True, vmem_limit_bytes=60 * 1024 * 1024
        ),
        name="exchange",
    )(row_perm, a_cols, b_cols, a_vals, b_vals)


def on_device(a_vals, a_cols, b_vals, b_cols, row_perm):
    got = exchange(
        row_perm,
        a_cols.reshape(ROWS, KA),
        b_cols.T,
        a_vals.reshape(ROWS * KA, TILE, TILE),
        b_vals.reshape(KWR * 2, TILE, TILE),
    )
    own_row = lax.axis_index("row")
    source = lax.dynamic_slice_in_dim(row_perm, own_row * ROWS, ROWS) // ROWS
    return got.at[source].get(mode="promise_in_bounds")


def solution(mesh):
    placed = (
        P("row", ("col", "layer"), None, None, None),
        P("row", ("col", "layer"), None),
        P(("col", "layer"), "row", None, None),
        P(("col", "layer"), "row"),
        P(),
    )
    return jax.shard_map(
        on_device,
        mesh=mesh,
        in_specs=placed,
        out_specs=P("row", ("col", "layer"), None, None),
        check_vma=False,
    )
```

```python
import functools

import jax
import jax.numpy as jnp
from jax import lax
from jax.experimental import pallas as pl
from jax.experimental.pallas import tpu as pltpu
from jax.sharding import PartitionSpec as P

TILE = 128
NC = 32
KWR = 24
KA = 12
ROWS = 8
RING = 4
CHUNK = 4
NCH = KWR // CHUNK
PIECE = CHUNK * 2
UNITS = NCH * 2
UNIT = PIECE // 2
HALF = UNIT // 2
AHEAD = 2
MINOR = ROWS // 2 * TILE
NB = 1024
NSTEP = NC * TILE // NB
TOP = 32767.0
UNROLL = 4
PHASES = (2, 1, 3, 0)
MESH = pl.DeviceIdType.MESH
ORDER = "F0 F1 N0 F2 N1 F3 N2 S0 N3 S1 L0 S2 L1 S3 L2 L3"


def encode(v):
    top = jnp.maximum(jnp.max(jnp.abs(v), axis=0, keepdims=True), 1e-30)
    coded = jnp.round(v * (TOP / top)).astype(jnp.int32).astype(jnp.int16)
    return coded, top * (1.0 / TOP)


def decode(coded, scale):
    return coded.astype(jnp.int32).astype(jnp.float32) * scale


def kernel(
    perm, ac_ref, bc_ref, a_hbm, b_hbm, out,
    a_v, b_v0, b_v1, b_v2, b_v3, b_v4, b_v5, ad, acc, ia_v, bc_v, ib_v, w_own, w_all, ia, ib,
    s1, s1s, r1, r1s, s2, s2s, r2, r2s, s3, s3s, r3, r3s, fin,
    g_send, g_recv, loc_sem, w_send, w_recv, m_send, m_recv, y_send, y_recv,
):
    b_v = (b_v0, b_v1, b_v2, b_v3, b_v4, b_v5)
    row = lax.axis_index("row")
    x = lax.axis_index("col")
    z = lax.axis_index("layer")
    y, c = row // 2, lax.rem(row, 2)

    def at_row(dy, dc):
        return lax.rem(y + dy, RING) * 2 + lax.rem(c + dc, 2)

    def dev_row(dy, dc):
        return (at_row(dy, dc), x, z)

    def dev_f(h, df):
        if h == 0:
            return (row, lax.rem(x + df, RING), z)
        return (row, x, lax.rem(z + df, RING))

    barrier = pltpu.get_barrier_semaphore()
    peers = [dev_row(dy, dc) for dy in range(RING) for dc in range(2) if dy or dc]
    peers += [dev_f(h, df) for h in range(2) for df in range(1, RING)]
    for peer in peers:
        pl.semaphore_signal(barrier, inc=1, device_id=peer, device_id_type=MESH)

    lane = lax.broadcasted_iota(jnp.int32, (ROWS, TILE), 1)
    left = lax.broadcasted_iota(jnp.int32, (ROWS, TILE), 0)
    table = jnp.full((ROWS, TILE), ROWS * KA, jnp.int32)
    for k in range(KA):
        table = jnp.where(ac_ref[:, k : k + 1] == lane, left * KA + k, table)
    ia_v[...] = table
    ia_copy = pltpu.make_async_copy(ia_v, ia, loc_sem.at[NCH + 1])
    ia_copy.start()
    bc_v[...] = jnp.full((ROWS, TILE), -1, jnp.int32)
    bc_v[0:2, 0:KWR] = bc_ref[...]
    col = lax.broadcasted_iota(jnp.int32, (NC, TILE), 0)
    inner = lax.rem(lax.broadcasted_iota(jnp.int32, (NC, TILE), 1), CHUNK)
    table = jnp.zeros((NC, TILE), jnp.int32)
    for k in range(2):
        table = jnp.where(bc_v[k : k + 1, :] == col, row * PIECE + inner * 2 + k + 1, table)
    w_own[...] = table

    a_copy = pltpu.make_async_copy(a_hbm, a_v.at[pl.ds(0, ROWS * KA)], loc_sem.at[NCH])
    a_copy.start()
    own = [
        pltpu.make_async_copy(
            b_hbm.at[pl.ds(q * PIECE, PIECE)], b_v[q].at[pl.ds(row * PIECE, PIECE)], loc_sem.at[q]
        )
        for q in range(NCH)
    ]
    for q in range(NCH):
        own[q].start()
    zero = jnp.zeros((TILE, TILE), jnp.bfloat16)
    a_v[ROWS * KA] = zero
    for q in range(NCH):
        b_v[q][ROWS * PIECE] = zero
    pl.semaphore_wait(barrier, len(peers))

    w_copies = [
        pltpu.make_async_remote_copy(
            src_ref=w_own,
            dst_ref=w_all.at[row],
            send_sem=w_send.at[2 * dy + dc],
            recv_sem=w_recv.at[2 * dy + dc],
            device_id=dev_row(dy, dc),
            device_id_type=MESH,
        )
        for dy in range(RING)
        for dc in range(2)
        if dy or dc
    ]
    for copy in w_copies:
        copy.start()

    def tables():
        w_all[row] = w_own[...]
        for copy in w_copies:
            copy.wait_recv()
        top = w_all[0]
        for source in range(1, ROWS):
            top = jnp.maximum(top, w_all[source])
        ib_v[...] = jnp.where(top > 0, top - 1, ROWS * PIECE)
        ib_copy = pltpu.make_async_copy(ib_v, ib, loc_sem.at[NCH + 2])
        ib_copy.start()
        ib_copy.wait()
        ia_copy.wait()

    def g_copy(u, kind, src, dst_at, n, target):
        return pltpu.make_async_remote_copy(
            src_ref=src,
            dst_ref=b_v[u // 2].at[pl.ds(dst_at, n)],
            send_sem=g_send.at[u, kind],
            recv_sem=g_recv.at[u, kind],
            device_id=target,
            device_id_type=MESH,
        )

    up, down, sib = dev_row(1, 0), dev_row(3, 0), dev_row(0, 1)

    def g_all(u):
        at_own, at_below, at_above, at_far = (
            at_row(d, 0) * PIECE + u % 2 * UNIT for d in (0, 3, 1, 2)
        )
        mine = b_hbm.at[pl.ds(u * UNIT, UNIT)]
        held = lambda at, n: b_v[u // 2].at[pl.ds(at, n)]
        return (
            g_copy(u, 0, mine, at_own, UNIT, up),
            g_copy(u, 1, mine, at_own, UNIT, down),
            g_copy(u, 2, mine, at_own, UNIT, sib),
            g_copy(u, 3, held(at_below, HALF), at_below, HALF, up),
            g_copy(u, 4, held(at_above + HALF, HALF), at_above + HALF, HALF, down),
            g_copy(u, 5, held(at_below, UNIT), at_below, UNIT, sib),
            g_copy(u, 6, held(at_above, UNIT), at_above, UNIT, sib),
            g_copy(u, 7, held(at_far, HALF), at_far, HALF, sib),
            g_copy(u, 8, held(at_far + HALF, HALF), at_far + HALF, HALF, sib),
        )

    copies = [g_all(u) for u in range(UNITS)]

    def first(u):
        for kind in (0, 1, 2):
            copies[u][kind].start()

    def relay(u):
        copies[u][0].wait_recv()
        copies[u][3].start()
        copies[u][5].start()
        copies[u][1].wait_recv()
        copies[u][4].start()
        copies[u][6].start()
        if u + AHEAD < UNITS:
            first(u + AHEAD)

    def pass_on(u):
        copies[u][3].wait_recv()
        copies[u][7].start()
        copies[u][4].wait_recv()
        copies[u][8].start()

    def arrived(q):
        own[q].wait()
        for u in (2 * q, 2 * q + 1):
            for kind in (2, 5, 6, 7, 8):
                copies[u][kind].wait_recv()

    def taken(j):
        total = jnp.int32(0)
        for i in range(ROWS):
            p = perm[j * ROWS + i]
            total = jnp.maximum(total, jnp.where(lax.div(p, ROWS) == row, lax.rem(p, ROWS), 0))
        return total

    def place(d):
        return d % 2 * MINOR + d // 2 * TILE

    def dense_a(q, rows):
        for d in range(ROWS):
            for k in range(CHUNK):
                ad[place(d) : place(d) + TILE, k * TILE : (k + 1) * TILE] = a_v[
                    ia[rows[d], q * CHUNK + k]
                ]

    def multiply(q, h, n, r0, count):
        def tile(k, i):
            col = n * 8 + i if h == 0 else (i // 2 * RING + n) * 2 + i % 2
            return b_v[q][ib[col, q * CHUNK + k]]

        right = jnp.concatenate(
            [jnp.concatenate([tile(k, i) for i in range(8)], axis=1) for k in range(CHUNK)], axis=0
        )
        cols = pl.ds(pl.multiple_of(n * NB, NB), NB)
        part = jnp.dot(ad[r0 : r0 + count, :], right, preferred_element_type=jnp.float32)
        if q == 0:
            acc[r0 : r0 + count, cols] = part
        else:
            acc[r0 : r0 + count, cols] = acc[r0 : r0 + count, cols] + part

    def chunk(q, hooks):
        @pl.loop(0, NSTEP)
        def _(n):
            for step, act in hooks:
                pl.when(n == step)(act)
            for h in range(2):
                multiply(q, h, n, h * MINOR, MINOR)

    def pos(h):
        return (x, z) if h == 0 else (z, x)

    def held_tile(d, f_at, s_at, cc):
        lanes = pl.ds(pl.multiple_of((f_at * RING + s_at) * 2 * TILE + cc * TILE, TILE), TILE)
        return (slice(place(d), place(d) + TILE), lanes)

    def m_copy(d, kind, src, dst, target):
        return pltpu.make_async_remote_copy(
            src_ref=src,
            dst_ref=dst,
            send_sem=m_send.at[d, kind],
            recv_sem=m_recv.at[d, kind],
            device_id=target,
            device_id_type=MESH,
        )

    def m_all(d, h):
        res = []
        for way in range(2):
            target = dev_f(h, 1 if way == 0 else 3)
            res.append(m_copy(d, 2 * way, s1.at[d, way], r1.at[d, way], target))
            res.append(m_copy(d, 2 * way + 1, s1s.at[d, way], r1s.at[d, way], target))
        for way in range(2):
            target = dev_f(h, 1 if way == 0 else 3)
            res.append(m_copy(d, 4 + 2 * way, s2.at[d, way], r2.at[d, way], target))
            res.append(m_copy(d, 5 + 2 * way, s2s.at[d, way], r2s.at[d, way], target))
        for ds in range(1, RING):
            target = dev_f(1 - h, ds)
            res.append(m_copy(d, 6 + 2 * ds, s3.at[d, ds - 1], r3.at[d, ds - 1], target))
            res.append(m_copy(d, 7 + 2 * ds, s3s.at[d, ds - 1], r3s.at[d, ds - 1], target))
        return res

    m = [m_all(d, d % 2) for d in range(ROWS)]

    def far_part(d):
        h = d % 2
        f, _ = pos(h)
        f2 = lax.rem(f + 2, RING)
        for way in range(2):

            @pl.loop(0, 4, unroll=UNROLL)
            def _(i):
                v = acc[held_tile(d, f2, way * 2 + i // 2, lax.rem(i, 2))]
                coded, scale = encode(v)
                s1[d, way, i] = coded
                s1s[d, way, pl.ds(i, 1), :] = scale

            m[d][2 * way].start()
            m[d][2 * way + 1].start()

    def near_part(d):
        h = d % 2
        f, _ = pos(h)
        for way in range(2):
            fd = lax.rem(f + (1 if way == 0 else 3), RING)
            m[d][2 * way].wait_recv()
            m[d][2 * way + 1].wait_recv()

            @pl.loop(0, 4, unroll=UNROLL)
            def _(i):
                v = acc[held_tile(d, fd, (1 - way) * 2 + i // 2, lax.rem(i, 2))]
                coded, scale = encode(v)
                s2[d, way, (1 - way) * 4 + i] = coded
                s2s[d, way, pl.ds((1 - way) * 4 + i, 1), :] = scale

            @pl.loop(0, 4, unroll=UNROLL)
            def _(i):
                v = acc[held_tile(d, fd, way * 2 + i // 2, lax.rem(i, 2))]
                v = v + decode(r1[d, way, i], r1s[d, way, pl.ds(i, 1), :])
                coded, scale = encode(v)
                s2[d, way, way * 4 + i] = coded
                s2s[d, way, pl.ds(way * 4 + i, 1), :] = scale

            m[d][4 + 2 * way].start()
            m[d][5 + 2 * way].start()

    def second(d):
        h = d % 2
        f, s = pos(h)
        for kind in range(4, 8):
            m[d][kind].wait_recv()
        for ds in (1, 2, 3, 0):
            s_at = lax.rem(s + ds, RING)

            @pl.loop(0, 2, unroll=2)
            def _(cc):
                where = held_tile(d, f, s_at, cc)
                i = s_at * 2 + cc
                v = (
                    acc[where]
                    + decode(r2[d, 0, i], r2s[d, 0, pl.ds(i, 1), :])
                    + decode(r2[d, 1, i], r2s[d, 1, pl.ds(i, 1), :])
                )
                if ds == 0:
                    fin[d, cc] = v
                else:
                    coded, scale = encode(v)
                    s3[d, ds - 1, cc] = coded
                    s3s[d, ds - 1, pl.ds(cc, 1), :] = scale

            if ds:
                m[d][6 + 2 * ds].start()
                m[d][7 + 2 * ds].start()

    y_copies = []
    for t, dy in enumerate(PHASES):
        for h in range(2):
            d = 2 * t + h
            if dy or h:
                y_copies.append(
                    pltpu.make_async_remote_copy(
                        src_ref=fin.at[d],
                        dst_ref=out.at[row],
                        send_sem=y_send.at[d],
                        recv_sem=y_recv.at[d],
                        device_id=dev_row(dy, h),
                        device_id_type=MESH,
                    )
                )
            else:
                y_copies.append(pltpu.make_async_copy(fin.at[d], out.at[row], y_send.at[d]))

    def last(d):
        for kind in range(8, 14):
            m[d][kind].wait_recv()

        @pl.loop(0, 2, unroll=2)
        def _(cc):
            v = fin[d, cc]
            for k in range(3):
                v = v + decode(r3[d, k, cc], r3s[d, k, pl.ds(cc, 1), :])
            fin[d, cc] = v

        y_copies[d].start()

    def both(step, t):
        step(2 * t)
        step(2 * t + 1)

    for u in range(AHEAD):
        first(u)
    tables()
    rows = [taken(at_row(dy, h)) for dy in PHASES for h in range(2)]
    relay(0)
    relay(1)
    pass_on(0)
    relay(2)
    pass_on(1)
    a_copy.wait()
    arrived(0)
    for q in range(NCH - 1):
        dense_a(q, rows)
        hooks = [(2, functools.partial(pass_on, 2 * q + 2))]
        hooks.append((1, functools.partial(relay, 2 * q + 3)))
        if 2 * q + 4 < UNITS:
            hooks.append((3, functools.partial(relay, 2 * q + 4)))
        chunk(q, hooks)
        pass_on(2 * q + 3)
        arrived(q + 1)
    dense_a(NCH - 1, rows)

    def ready(t):
        for h in range(2):
            f, _ = pos(h)
            multiply(NCH - 1, h, lax.rem(f + 2, RING), place(2 * t + h), TILE)
            far_part(2 * t + h)
        for h in range(2):
            f, _ = pos(h)

            @pl.loop(0, NSTEP - 1)
            def _(i):
                multiply(NCH - 1, h, lax.rem(f + 3 + i, RING), place(2 * t + h), TILE)

    def sent():
        for copy in w_copies:
            copy.wait_send()
        for u in range(UNITS):
            for copy in copies[u]:
                copy.wait_send()

    def sent_part(t, kinds):
        for d in (2 * t, 2 * t + 1):
            for kind in kinds:
                m[d][kind].wait_send()

    near = functools.partial(both, near_part)
    across = functools.partial(both, second)
    finish = functools.partial(both, last)

    steps = {"F": ready, "N": near, "S": across, "L": finish}
    for word in ORDER.split():
        t = int(word[1])
        if word == "S0":
            sent()
        if word[0] == "L":
            sent_part(t, range(8))
        steps[word[0]](t)
    for t in range(ROWS // 2):
        sent_part(t, range(8, 14))
    for copy in y_copies:
        copy.wait()


def exchange(row_perm, a_cols, b_cols, a_vals, b_vals):
    bf16, f32, i16, i32 = jnp.bfloat16, jnp.float32, jnp.int16, jnp.int32
    t2 = (TILE, TILE)
    b_chunk = pltpu.VMEM((ROWS * PIECE + 1, *t2), bf16)
    dma = pltpu.SemaphoreType.DMA
    return pl.pallas_call(
        kernel,
        out_shape=jax.ShapeDtypeStruct((ROWS, 2, *t2), f32),
        in_specs=[
            pl.BlockSpec(memory_space=pltpu.SMEM),
            pl.BlockSpec(memory_space=pltpu.VMEM),
            pl.BlockSpec(memory_space=pltpu.VMEM),
            pl.BlockSpec(memory_space=pl.ANY),
            pl.BlockSpec(memory_space=pl.ANY),
        ],
        out_specs=pl.BlockSpec(memory_space=pl.ANY),
        scratch_shapes=[
            pltpu.VMEM((ROWS * KA + 1, *t2), bf16),
            b_chunk, b_chunk, b_chunk, b_chunk, b_chunk, b_chunk,
            pltpu.VMEM((ROWS * TILE, CHUNK * TILE), bf16),
            pltpu.VMEM((ROWS * TILE, NC * TILE), f32),
            pltpu.VMEM((ROWS, TILE), i32),
            pltpu.VMEM((ROWS, TILE), i32),
            pltpu.VMEM((NC, TILE), i32),
            pltpu.VMEM((NC, TILE), i32),
            pltpu.VMEM((ROWS, NC, TILE), i32),
            pltpu.SMEM((ROWS, TILE), i32),
            pltpu.SMEM((NC, TILE), i32),
            pltpu.VMEM((ROWS, 2, 4, *t2), i16),
            pltpu.VMEM((ROWS, 2, 8, TILE), f32),
            pltpu.VMEM((ROWS, 2, 4, *t2), i16),
            pltpu.VMEM((ROWS, 2, 8, TILE), f32),
            pltpu.VMEM((ROWS, 2, 8, *t2), i16),
            pltpu.VMEM((ROWS, 2, 8, TILE), f32),
            pltpu.VMEM((ROWS, 2, 8, *t2), i16),
            pltpu.VMEM((ROWS, 2, 8, TILE), f32),
            pltpu.VMEM((ROWS, 3, 2, *t2), i16),
            pltpu.VMEM((ROWS, 3, 8, TILE), f32),
            pltpu.VMEM((ROWS, 3, 2, *t2), i16),
            pltpu.VMEM((ROWS, 3, 8, TILE), f32),
            pltpu.VMEM((ROWS, 2, *t2), f32),
            dma((UNITS, 9)), dma((UNITS, 9)), dma((NCH + 3,)), dma((ROWS,)), dma((ROWS,)),
            dma((ROWS, 14)), dma((ROWS, 14)), dma((ROWS,)), dma((ROWS,)),
        ],
        compiler_params=pltpu.CompilerParams(
            collective_id=0, has_side_effects=True, vmem_limit_bytes=60 * 1024 * 1024
        ),
        name="exchange",
    )(row_perm, a_cols, b_cols, a_vals, b_vals)


def on_device(a_vals, a_cols, b_vals, b_cols, row_perm):
    got = exchange(
        row_perm,
        a_cols.reshape(ROWS, KA),
        b_cols.T,
        a_vals.reshape(ROWS * KA, TILE, TILE),
        b_vals.reshape(KWR * 2, TILE, TILE),
    )
    own_row = lax.axis_index("row")
    source = lax.dynamic_slice_in_dim(row_perm, own_row * ROWS, ROWS) // ROWS
    return got.at[source].get(mode="promise_in_bounds")


def solution(mesh):
    placed = (
        P("row", ("col", "layer"), None, None, None),
        P("row", ("col", "layer"), None),
        P(("col", "layer"), "row", None, None),
        P(("col", "layer"), "row"),
        P(),
    )
    return jax.shard_map(
        on_device,
        mesh=mesh,
        in_specs=placed,
        out_specs=P("row", ("col", "layer"), None, None),
        check_vma=False,
    )
```

```python
import functools

import jax
import jax.numpy as jnp
from jax import lax
from jax.experimental import pallas as pl
from jax.experimental.pallas import tpu as pltpu
from jax.sharding import PartitionSpec as P

TILE = 128
NC = 32
KWR = 24
KA = 12
ROWS = 8
RING = 4
CHUNK = 4
NCH = KWR // CHUNK
PIECE = CHUNK * 2
UNITS = NCH * 2
UNIT = PIECE // 2
HALF = UNIT // 2
AHEAD = 2
MINOR = ROWS // 2 * TILE
NB = 1024
NSTEP = NC * TILE // NB
TOP = 32767.0
UNROLL = 4
PHASES = (2, 1, 3, 0)
MESH = pl.DeviceIdType.MESH
ORDER = (
    ("F", 0), ("F", 1), ("N", 0), ("F", 2), ("N", 1), ("F", 3), ("N", 2), ("S", 0),
    ("N", 3), ("S", 1), ("L", 0), ("S", 2), ("L", 1), ("S", 3), ("L", 2), ("L", 3),
)


def encode(v):
    top = jnp.maximum(jnp.max(jnp.abs(v), axis=0, keepdims=True), 1e-30)
    coded = jnp.round(v * (TOP / top)).astype(jnp.int32).astype(jnp.int16)
    return coded, top * (1.0 / TOP)


def decode(coded, scale):
    return coded.astype(jnp.int32).astype(jnp.float32) * scale


def kernel(
    perm, ac_ref, bc_ref, a_hbm, b_hbm, out,
    a_v, b_v0, b_v1, b_v2, b_v3, b_v4, b_v5, ad, acc, ia_v, bc_v, ib_v, w_own, w_all, ia, ib,
    s1, s1s, r1, r1s, s2, s2s, r2, r2s, s3, s3s, r3, r3s, fin,
    g_send, g_recv, loc_sem, w_send, w_recv, m_send, m_recv, y_send, y_recv,
):
    b_v = (b_v0, b_v1, b_v2, b_v3, b_v4, b_v5)
    row = lax.axis_index("row")
    x = lax.axis_index("col")
    z = lax.axis_index("layer")
    y, c = row // 2, lax.rem(row, 2)

    def at_row(dy, dc):
        return lax.rem(y + dy, RING) * 2 + lax.rem(c + dc, 2)

    def dev_row(dy, dc):
        return (at_row(dy, dc), x, z)

    def dev_f(h, df):
        if h == 0:
            return (row, lax.rem(x + df, RING), z)
        return (row, x, lax.rem(z + df, RING))

    barrier = pltpu.get_barrier_semaphore()
    peers = [dev_row(dy, dc) for dy in range(RING) for dc in range(2) if dy or dc]
    peers += [dev_f(h, df) for h in range(2) for df in range(1, RING)]
    for peer in peers:
        pl.semaphore_signal(barrier, inc=1, device_id=peer, device_id_type=MESH)

    lane = lax.broadcasted_iota(jnp.int32, (ROWS, TILE), 1)
    left = lax.broadcasted_iota(jnp.int32, (ROWS, TILE), 0)
    table = jnp.full((ROWS, TILE), ROWS * KA, jnp.int32)
    for k in range(KA):
        table = jnp.where(ac_ref[:, k : k + 1] == lane, left * KA + k, table)
    ia_v[...] = table
    ia_copy = pltpu.make_async_copy(ia_v, ia, loc_sem.at[NCH + 1])
    ia_copy.start()
    bc_v[...] = jnp.full((ROWS, TILE), -1, jnp.int32)
    bc_v[0:2, 0:KWR] = bc_ref[...]
    col = lax.broadcasted_iota(jnp.int32, (NC, TILE), 0)
    inner = lax.rem(lax.broadcasted_iota(jnp.int32, (NC, TILE), 1), CHUNK)
    table = jnp.zeros((NC, TILE), jnp.int32)
    for k in range(2):
        table = jnp.where(bc_v[k : k + 1, :] == col, row * PIECE + inner * 2 + k + 1, table)
    w_own[...] = table

    a_copy = pltpu.make_async_copy(a_hbm, a_v.at[pl.ds(0, ROWS * KA)], loc_sem.at[NCH])
    a_copy.start()
    own = [
        pltpu.make_async_copy(
            b_hbm.at[pl.ds(q * PIECE, PIECE)], b_v[q].at[pl.ds(row * PIECE, PIECE)], loc_sem.at[q]
        )
        for q in range(NCH)
    ]
    for q in range(NCH):
        own[q].start()
    zero = jnp.zeros((TILE, TILE), jnp.bfloat16)
    a_v[ROWS * KA] = zero
    for q in range(NCH):
        b_v[q][ROWS * PIECE] = zero
    pl.semaphore_wait(barrier, len(peers))

    w_copies = [
        pltpu.make_async_remote_copy(
            src_ref=w_own,
            dst_ref=w_all.at[row],
            send_sem=w_send.at[2 * dy + dc],
            recv_sem=w_recv.at[2 * dy + dc],
            device_id=dev_row(dy, dc),
            device_id_type=MESH,
        )
        for dy in range(RING)
        for dc in range(2)
        if dy or dc
    ]
    for copy in w_copies:
        copy.start()

    def tables():
        w_all[row] = w_own[...]
        for copy in w_copies:
            copy.wait_recv()
        top = w_all[0]
        for source in range(1, ROWS):
            top = jnp.maximum(top, w_all[source])
        ib_v[...] = jnp.where(top > 0, top - 1, ROWS * PIECE)
        ib_copy = pltpu.make_async_copy(ib_v, ib, loc_sem.at[NCH + 2])
        ib_copy.start()
        ib_copy.wait()
        ia_copy.wait()

    def g_copy(u, kind, src, dst_at, n, target):
        return pltpu.make_async_remote_copy(
            src_ref=src,
            dst_ref=b_v[u // 2].at[pl.ds(dst_at, n)],
            send_sem=g_send.at[u, kind],
            recv_sem=g_recv.at[u, kind],
            device_id=target,
            device_id_type=MESH,
        )

    up, down, sib = dev_row(1, 0), dev_row(3, 0), dev_row(0, 1)

    def g_all(u):
        at_own, at_below, at_above, at_far = (
            at_row(d, 0) * PIECE + u % 2 * UNIT for d in (0, 3, 1, 2)
        )
        mine = b_hbm.at[pl.ds(u * UNIT, UNIT)]
        held = lambda at, n: b_v[u // 2].at[pl.ds(at, n)]
        return (
            g_copy(u, 0, mine, at_own, UNIT, up),
            g_copy(u, 1, mine, at_own, UNIT, down),
            g_copy(u, 2, mine, at_own, UNIT, sib),
            g_copy(u, 3, held(at_below, HALF), at_below, HALF, up),
            g_copy(u, 4, held(at_above + HALF, HALF), at_above + HALF, HALF, down),
            g_copy(u, 5, held(at_below, UNIT), at_below, UNIT, sib),
            g_copy(u, 6, held(at_above, UNIT), at_above, UNIT, sib),
            g_copy(u, 7, held(at_far, HALF), at_far, HALF, sib),
            g_copy(u, 8, held(at_far + HALF, HALF), at_far + HALF, HALF, sib),
        )

    copies = [g_all(u) for u in range(UNITS)]

    def first(u):
        for kind in (0, 1, 2):
            copies[u][kind].start()

    def relay(u):
        copies[u][0].wait_recv()
        copies[u][3].start()
        copies[u][5].start()
        copies[u][1].wait_recv()
        copies[u][4].start()
        copies[u][6].start()
        if u + AHEAD < UNITS:
            first(u + AHEAD)

    def pass_on(u):
        copies[u][3].wait_recv()
        copies[u][7].start()
        copies[u][4].wait_recv()
        copies[u][8].start()

    def arrived(q):
        own[q].wait()
        for u in (2 * q, 2 * q + 1):
            for kind in (2, 5, 6, 7, 8):
                copies[u][kind].wait_recv()

    def taken(j):
        total = jnp.int32(0)
        for i in range(ROWS):
            p = perm[j * ROWS + i]
            total = jnp.maximum(total, jnp.where(lax.div(p, ROWS) == row, lax.rem(p, ROWS), 0))
        return total

    def place(d):
        return d % 2 * MINOR + d // 2 * TILE

    def dense_a(q, rows):
        for d in range(ROWS):
            for k in range(CHUNK):
                ad[place(d) : place(d) + TILE, k * TILE : (k + 1) * TILE] = a_v[
                    ia[rows[d], q * CHUNK + k]
                ]

    def multiply(q, h, n, r0, count):
        def tile(k, i):
            col = n * 8 + i if h == 0 else (i // 2 * RING + n) * 2 + i % 2
            return b_v[q][ib[col, q * CHUNK + k]]

        right = jnp.concatenate(
            [jnp.concatenate([tile(k, i) for i in range(8)], axis=1) for k in range(CHUNK)], axis=0
        )
        cols = pl.ds(pl.multiple_of(n * NB, NB), NB)
        part = jnp.dot(ad[r0 : r0 + count, :], right, preferred_element_type=jnp.float32)
        if q == 0:
            acc[r0 : r0 + count, cols] = part
        else:
            acc[r0 : r0 + count, cols] = acc[r0 : r0 + count, cols] + part

    def chunk(q, hooks):
        @pl.loop(0, NSTEP)
        def _(n):
            for step, act in hooks:
                pl.when(n == step)(act)
            for h in range(2):
                multiply(q, h, n, h * MINOR, MINOR)

    def pos(h):
        return (x, z) if h == 0 else (z, x)

    def held_tile(d, f_at, s_at, cc):
        lanes = pl.ds(pl.multiple_of((f_at * RING + s_at) * 2 * TILE + cc * TILE, TILE), TILE)
        return (slice(place(d), place(d) + TILE), lanes)

    def m_copy(d, kind, src, dst, target):
        return pltpu.make_async_remote_copy(
            src_ref=src,
            dst_ref=dst,
            send_sem=m_send.at[d, kind],
            recv_sem=m_recv.at[d, kind],
            device_id=target,
            device_id_type=MESH,
        )

    def m_all(d, h):
        res = []
        for way in range(2):
            target = dev_f(h, 1 if way == 0 else 3)
            res.append(m_copy(d, 2 * way, s1.at[d, way], r1.at[d, way], target))
            res.append(m_copy(d, 2 * way + 1, s1s.at[d, way], r1s.at[d, way], target))
        for way in range(2):
            target = dev_f(h, 1 if way == 0 else 3)
            res.append(m_copy(d, 4 + 2 * way, s2.at[d, way], r2.at[d, way], target))
            res.append(m_copy(d, 5 + 2 * way, s2s.at[d, way], r2s.at[d, way], target))
        for ds in range(1, RING):
            target = dev_f(1 - h, ds)
            res.append(m_copy(d, 6 + 2 * ds, s3.at[d, ds - 1], r3.at[d, ds - 1], target))
            res.append(m_copy(d, 7 + 2 * ds, s3s.at[d, ds - 1], r3s.at[d, ds - 1], target))
        return res

    m = [m_all(d, d % 2) for d in range(ROWS)]

    def far_part(d):
        h = d % 2
        f, _ = pos(h)
        f2 = lax.rem(f + 2, RING)
        for way in range(2):

            @pl.loop(0, 4, unroll=UNROLL)
            def _(i):
                v = acc[held_tile(d, f2, way * 2 + i // 2, lax.rem(i, 2))]
                coded, scale = encode(v)
                s1[d, way, i] = coded
                s1s[d, way, pl.ds(i, 1), :] = scale

            m[d][2 * way].start()
            m[d][2 * way + 1].start()

    def near_part(d):
        h = d % 2
        f, _ = pos(h)
        for way in range(2):
            fd = lax.rem(f + (1 if way == 0 else 3), RING)
            m[d][2 * way].wait_recv()
            m[d][2 * way + 1].wait_recv()

            @pl.loop(0, 4, unroll=UNROLL)
            def _(i):
                v = acc[held_tile(d, fd, (1 - way) * 2 + i // 2, lax.rem(i, 2))]
                coded, scale = encode(v)
                s2[d, way, (1 - way) * 4 + i] = coded
                s2s[d, way, pl.ds((1 - way) * 4 + i, 1), :] = scale

            @pl.loop(0, 4, unroll=UNROLL)
            def _(i):
                v = acc[held_tile(d, fd, way * 2 + i // 2, lax.rem(i, 2))]
                v = v + decode(r1[d, way, i], r1s[d, way, pl.ds(i, 1), :])
                coded, scale = encode(v)
                s2[d, way, way * 4 + i] = coded
                s2s[d, way, pl.ds(way * 4 + i, 1), :] = scale

            m[d][4 + 2 * way].start()
            m[d][5 + 2 * way].start()

    def second(d):
        h = d % 2
        f, s = pos(h)
        for kind in range(4, 8):
            m[d][kind].wait_recv()
        for ds in (1, 2, 3, 0):
            s_at = lax.rem(s + ds, RING)

            @pl.loop(0, 2, unroll=2)
            def _(cc):
                where = held_tile(d, f, s_at, cc)
                i = s_at * 2 + cc
                v = (
                    acc[where]
                    + decode(r2[d, 0, i], r2s[d, 0, pl.ds(i, 1), :])
                    + decode(r2[d, 1, i], r2s[d, 1, pl.ds(i, 1), :])
                )
                if ds == 0:
                    fin[d, cc] = v
                else:
                    coded, scale = encode(v)
                    s3[d, ds - 1, cc] = coded
                    s3s[d, ds - 1, pl.ds(cc, 1), :] = scale

            if ds:
                m[d][6 + 2 * ds].start()
                m[d][7 + 2 * ds].start()

    y_copies = []
    for t, dy in enumerate(PHASES):
        for h in range(2):
            d = 2 * t + h
            if dy or h:
                y_copies.append(
                    pltpu.make_async_remote_copy(
                        src_ref=fin.at[d],
                        dst_ref=out.at[row],
                        send_sem=y_send.at[d],
                        recv_sem=y_recv.at[d],
                        device_id=dev_row(dy, h),
                        device_id_type=MESH,
                    )
                )
            else:
                y_copies.append(pltpu.make_async_copy(fin.at[d], out.at[row], y_send.at[d]))

    def last(d):
        for kind in range(8, 14):
            m[d][kind].wait_recv()

        @pl.loop(0, 2, unroll=2)
        def _(cc):
            v = fin[d, cc]
            for k in range(3):
                v = v + decode(r3[d, k, cc], r3s[d, k, pl.ds(cc, 1), :])
            fin[d, cc] = v

        y_copies[d].start()

    def both(step, t):
        step(2 * t)
        step(2 * t + 1)

    for u in range(AHEAD):
        first(u)
    tables()
    rows = [taken(at_row(dy, h)) for dy in PHASES for h in range(2)]
    relay(0)
    relay(1)
    pass_on(0)
    relay(2)
    pass_on(1)
    a_copy.wait()
    arrived(0)
    for q in range(NCH - 1):
        dense_a(q, rows)
        hooks = [(2, functools.partial(pass_on, 2 * q + 2))]
        hooks.append((1, functools.partial(relay, 2 * q + 3)))
        if 2 * q + 4 < UNITS:
            hooks.append((3, functools.partial(relay, 2 * q + 4)))
        chunk(q, hooks)
        pass_on(2 * q + 3)
        arrived(q + 1)
    dense_a(NCH - 1, rows)

    def ready(t):
        for h in range(2):
            f, _ = pos(h)
            multiply(NCH - 1, h, lax.rem(f + 2, RING), place(2 * t + h), TILE)
            far_part(2 * t + h)
        for h in range(2):
            f, _ = pos(h)

            @pl.loop(0, NSTEP - 1)
            def _(i):
                multiply(NCH - 1, h, lax.rem(f + 3 + i, RING), place(2 * t + h), TILE)

    def sent():
        for copy in w_copies:
            copy.wait_send()
        for u in range(UNITS):
            for copy in copies[u]:
                copy.wait_send()

    def sent_part(t, kinds):
        for d in (2 * t, 2 * t + 1):
            for kind in kinds:
                m[d][kind].wait_send()

    near = functools.partial(both, near_part)
    across = functools.partial(both, second)
    finish = functools.partial(both, last)

    steps = {"F": ready, "N": near, "S": across, "L": finish}
    for step, t in ORDER:
        if step == "S" and t == 0:
            sent()
        if step == "L":
            sent_part(t, range(8))
        steps[step](t)
    for t in range(ROWS // 2):
        sent_part(t, range(8, 14))
    for copy in y_copies:
        copy.wait()


def exchange(row_perm, a_cols, b_cols, a_vals, b_vals):
    bf16, f32, i16, i32 = jnp.bfloat16, jnp.float32, jnp.int16, jnp.int32
    t2 = (TILE, TILE)
    b_chunk = pltpu.VMEM((ROWS * PIECE + 1, *t2), bf16)
    dma = pltpu.SemaphoreType.DMA
    return pl.pallas_call(
        kernel,
        out_shape=jax.ShapeDtypeStruct((ROWS, 2, *t2), f32),
        in_specs=[
            pl.BlockSpec(memory_space=pltpu.SMEM),
            pl.BlockSpec(memory_space=pltpu.VMEM),
            pl.BlockSpec(memory_space=pltpu.VMEM),
            pl.BlockSpec(memory_space=pl.ANY),
            pl.BlockSpec(memory_space=pl.ANY),
        ],
        out_specs=pl.BlockSpec(memory_space=pl.ANY),
        scratch_shapes=[
            pltpu.VMEM((ROWS * KA + 1, *t2), bf16),
            b_chunk, b_chunk, b_chunk, b_chunk, b_chunk, b_chunk,
            pltpu.VMEM((ROWS * TILE, CHUNK * TILE), bf16),
            pltpu.VMEM((ROWS * TILE, NC * TILE), f32),
            pltpu.VMEM((ROWS, TILE), i32),
            pltpu.VMEM((ROWS, TILE), i32),
            pltpu.VMEM((NC, TILE), i32),
            pltpu.VMEM((NC, TILE), i32),
            pltpu.VMEM((ROWS, NC, TILE), i32),
            pltpu.SMEM((ROWS, TILE), i32),
            pltpu.SMEM((NC, TILE), i32),
            pltpu.VMEM((ROWS, 2, 4, *t2), i16),
            pltpu.VMEM((ROWS, 2, 8, TILE), f32),
            pltpu.VMEM((ROWS, 2, 4, *t2), i16),
            pltpu.VMEM((ROWS, 2, 8, TILE), f32),
            pltpu.VMEM((ROWS, 2, 8, *t2), i16),
            pltpu.VMEM((ROWS, 2, 8, TILE), f32),
            pltpu.VMEM((ROWS, 2, 8, *t2), i16),
            pltpu.VMEM((ROWS, 2, 8, TILE), f32),
            pltpu.VMEM((ROWS, 3, 2, *t2), i16),
            pltpu.VMEM((ROWS, 3, 8, TILE), f32),
            pltpu.VMEM((ROWS, 3, 2, *t2), i16),
            pltpu.VMEM((ROWS, 3, 8, TILE), f32),
            pltpu.VMEM((ROWS, 2, *t2), f32),
            dma((UNITS, 9)), dma((UNITS, 9)), dma((NCH + 3,)), dma((ROWS,)), dma((ROWS,)),
            dma((ROWS, 14)), dma((ROWS, 14)), dma((ROWS,)), dma((ROWS,)),
        ],
        compiler_params=pltpu.CompilerParams(
            collective_id=0, has_side_effects=True, vmem_limit_bytes=60 * 1024 * 1024
        ),
        name="exchange",
    )(row_perm, a_cols, b_cols, a_vals, b_vals)


def on_device(a_vals, a_cols, b_vals, b_cols, row_perm):
    got = exchange(
        row_perm,
        a_cols.reshape(ROWS, KA),
        b_cols.T,
        a_vals.reshape(ROWS * KA, TILE, TILE),
        b_vals.reshape(KWR * 2, TILE, TILE),
    )
    own_row = lax.axis_index("row")
    source = lax.dynamic_slice_in_dim(row_perm, own_row * ROWS, ROWS) // ROWS
    return got.at[source].get(mode="promise_in_bounds")


def solution(mesh):
    placed = (
        P("row", ("col", "layer"), None, None, None),
        P("row", ("col", "layer"), None),
        P(("col", "layer"), "row", None, None),
        P(("col", "layer"), "row"),
        P(),
    )
    return jax.shard_map(
        on_device,
        mesh=mesh,
        in_specs=placed,
        out_specs=P("row", ("col", "layer"), None, None),
        check_vma=False,
    )
```

```python
import functools

import jax
import jax.numpy as jnp
from jax import lax
from jax.experimental import pallas as pl
from jax.experimental.pallas import tpu as pltpu
from jax.sharding import PartitionSpec as P

TILE = 128
NC = 32
KWR = 24
KA = 12
ROWS = 8
RING = 4
CHUNK = 4
NCH = KWR // CHUNK
PIECE = CHUNK * 2
UNITS = NCH * 2
UNIT = PIECE // 2
HALF = UNIT // 2
AHEAD = 2
MINOR = ROWS // 2 * TILE
NB = 1024
NSTEP = NC * TILE // NB
TOP = 32767.0
UNROLL = 4
DEST = ((2, 0), (2, 1), (1, 0), (3, 0), (1, 1), (3, 1), (0, 0), (0, 1))
MESH = pl.DeviceIdType.MESH
ORDER = (
    ("F", 0), ("F", 1), ("N", 0), ("F", 2), ("N", 1), ("F", 3), ("N", 2), ("S", 0),
    ("N", 3), ("S", 1), ("L", 0), ("S", 2), ("L", 1), ("S", 3), ("L", 2), ("L", 3),
)


def encode(v):
    top = jnp.maximum(jnp.max(jnp.abs(v), axis=0, keepdims=True), 1e-30)
    coded = jnp.round(v * (TOP / top)).astype(jnp.int32).astype(jnp.int16)
    return coded, top * (1.0 / TOP)


def decode(coded, scale):
    return coded.astype(jnp.int32).astype(jnp.float32) * scale


def kernel(
    perm, ac_ref, bc_ref, a_hbm, b_hbm, out,
    a_v, b_v0, b_v1, b_v2, b_v3, b_v4, b_v5, ad, acc, ia_v, bc_v, ib_v, w_own, w_all, ia, ib,
    s1, s1s, r1, r1s, s2, s2s, r2, r2s, s3, s3s, r3, r3s, fin,
    g_send, g_recv, loc_sem, w_send, w_recv, m_send, m_recv, y_send, y_recv,
):
    b_v = (b_v0, b_v1, b_v2, b_v3, b_v4, b_v5)
    row = lax.axis_index("row")
    x = lax.axis_index("col")
    z = lax.axis_index("layer")
    y, c = row // 2, lax.rem(row, 2)

    def at_row(dy, dc):
        return lax.rem(y + dy, RING) * 2 + lax.rem(c + dc, 2)

    def dev_row(dy, dc):
        return (at_row(dy, dc), x, z)

    def dev_f(h, df):
        if h == 0:
            return (row, lax.rem(x + df, RING), z)
        return (row, x, lax.rem(z + df, RING))

    barrier = pltpu.get_barrier_semaphore()
    peers = [dev_row(dy, dc) for dy in range(RING) for dc in range(2) if dy or dc]
    peers += [dev_f(h, df) for h in range(2) for df in range(1, RING)]
    for peer in peers:
        pl.semaphore_signal(barrier, inc=1, device_id=peer, device_id_type=MESH)

    lane = lax.broadcasted_iota(jnp.int32, (ROWS, TILE), 1)
    left = lax.broadcasted_iota(jnp.int32, (ROWS, TILE), 0)
    table = jnp.full((ROWS, TILE), ROWS * KA, jnp.int32)
    for k in range(KA):
        table = jnp.where(ac_ref[:, k : k + 1] == lane, left * KA + k, table)
    ia_v[...] = table
    ia_copy = pltpu.make_async_copy(ia_v, ia, loc_sem.at[NCH + 1])
    ia_copy.start()
    bc_v[...] = jnp.full((ROWS, TILE), -1, jnp.int32)
    bc_v[0:2, 0:KWR] = bc_ref[...]
    col = lax.broadcasted_iota(jnp.int32, (NC, TILE), 0)
    inner = lax.rem(lax.broadcasted_iota(jnp.int32, (NC, TILE), 1), CHUNK)
    table = jnp.zeros((NC, TILE), jnp.int32)
    for k in range(2):
        table = jnp.where(bc_v[k : k + 1, :] == col, row * PIECE + inner * 2 + k + 1, table)
    w_own[...] = table

    a_copy = pltpu.make_async_copy(a_hbm, a_v.at[pl.ds(0, ROWS * KA)], loc_sem.at[NCH])
    a_copy.start()
    own = [
        pltpu.make_async_copy(
            b_hbm.at[pl.ds(q * PIECE, PIECE)], b_v[q].at[pl.ds(row * PIECE, PIECE)], loc_sem.at[q]
        )
        for q in range(NCH)
    ]
    for q in range(NCH):
        own[q].start()
    zero = jnp.zeros((TILE, TILE), jnp.bfloat16)
    a_v[ROWS * KA] = zero
    for q in range(NCH):
        b_v[q][ROWS * PIECE] = zero
    pl.semaphore_wait(barrier, len(peers))

    w_copies = [
        pltpu.make_async_remote_copy(
            src_ref=w_own,
            dst_ref=w_all.at[row],
            send_sem=w_send.at[2 * dy + dc],
            recv_sem=w_recv.at[2 * dy + dc],
            device_id=dev_row(dy, dc),
            device_id_type=MESH,
        )
        for dy in range(RING)
        for dc in range(2)
        if dy or dc
    ]
    for copy in w_copies:
        copy.start()

    def tables():
        w_all[row] = w_own[...]
        for copy in w_copies:
            copy.wait_recv()
        top = w_all[0]
        for source in range(1, ROWS):
            top = jnp.maximum(top, w_all[source])
        ib_v[...] = jnp.where(top > 0, top - 1, ROWS * PIECE)
        ib_copy = pltpu.make_async_copy(ib_v, ib, loc_sem.at[NCH + 2])
        ib_copy.start()
        ib_copy.wait()
        ia_copy.wait()

    def g_copy(u, kind, src, dst_at, n, target):
        return pltpu.make_async_remote_copy(
            src_ref=src,
            dst_ref=b_v[u // 2].at[pl.ds(dst_at, n)],
            send_sem=g_send.at[u, kind],
            recv_sem=g_recv.at[u, kind],
            device_id=target,
            device_id_type=MESH,
        )

    up, down, sib = dev_row(1, 0), dev_row(3, 0), dev_row(0, 1)

    def g_all(u):
        at_own, at_below, at_above, at_far = (
            at_row(d, 0) * PIECE + u % 2 * UNIT for d in (0, 3, 1, 2)
        )
        mine = b_hbm.at[pl.ds(u * UNIT, UNIT)]
        held = lambda at, n: b_v[u // 2].at[pl.ds(at, n)]
        return (
            g_copy(u, 0, mine, at_own, UNIT, up),
            g_copy(u, 1, mine, at_own, UNIT, down),
            g_copy(u, 2, mine, at_own, UNIT, sib),
            g_copy(u, 3, held(at_below, HALF), at_below, HALF, up),
            g_copy(u, 4, held(at_above + HALF, HALF), at_above + HALF, HALF, down),
            g_copy(u, 5, held(at_below, UNIT), at_below, UNIT, sib),
            g_copy(u, 6, held(at_above, UNIT), at_above, UNIT, sib),
            g_copy(u, 7, held(at_far, HALF), at_far, HALF, sib),
            g_copy(u, 8, held(at_far + HALF, HALF), at_far + HALF, HALF, sib),
        )

    copies = [g_all(u) for u in range(UNITS)]

    def first(u):
        for kind in (0, 1, 2):
            copies[u][kind].start()

    def relay(u):
        copies[u][0].wait_recv()
        copies[u][3].start()
        copies[u][5].start()
        copies[u][1].wait_recv()
        copies[u][4].start()
        copies[u][6].start()
        if u + AHEAD < UNITS:
            first(u + AHEAD)

    def pass_on(u):
        copies[u][3].wait_recv()
        copies[u][7].start()
        copies[u][4].wait_recv()
        copies[u][8].start()

    def arrived(q):
        own[q].wait()
        for u in (2 * q, 2 * q + 1):
            for kind in (2, 5, 6, 7, 8):
                copies[u][kind].wait_recv()

    def taken(j):
        total = jnp.int32(0)
        for i in range(ROWS):
            p = perm[j * ROWS + i]
            total = jnp.maximum(total, jnp.where(lax.div(p, ROWS) == row, lax.rem(p, ROWS), 0))
        return total

    def place(d):
        return d % 2 * MINOR + d // 2 * TILE

    def dense_a(q, rows):
        for d in range(ROWS):
            for k in range(CHUNK):
                ad[place(d) : place(d) + TILE, k * TILE : (k + 1) * TILE] = a_v[
                    ia[rows[d], q * CHUNK + k]
                ]

    def multiply(q, h, n, r0, count):
        def tile(k, i):
            col = n * 8 + i if h == 0 else (i // 2 * RING + n) * 2 + i % 2
            return b_v[q][ib[col, q * CHUNK + k]]

        right = jnp.concatenate(
            [jnp.concatenate([tile(k, i) for i in range(8)], axis=1) for k in range(CHUNK)], axis=0
        )
        cols = pl.ds(pl.multiple_of(n * NB, NB), NB)
        part = jnp.dot(ad[r0 : r0 + count, :], right, preferred_element_type=jnp.float32)
        if q == 0:
            acc[r0 : r0 + count, cols] = part
        else:
            acc[r0 : r0 + count, cols] = acc[r0 : r0 + count, cols] + part

    def chunk(q, hooks):
        @pl.loop(0, NSTEP)
        def _(n):
            for step, act in hooks:
                pl.when(n == step)(act)
            for h in range(2):
                multiply(q, h, n, h * MINOR, MINOR)

    def pos(h):
        return (x, z) if h == 0 else (z, x)

    def held_tile(d, f_at, s_at, cc):
        lanes = pl.ds(pl.multiple_of((f_at * RING + s_at) * 2 * TILE + cc * TILE, TILE), TILE)
        return (slice(place(d), place(d) + TILE), lanes)

    def m_copy(d, kind, src, dst, target):
        return pltpu.make_async_remote_copy(
            src_ref=src,
            dst_ref=dst,
            send_sem=m_send.at[d, kind],
            recv_sem=m_recv.at[d, kind],
            device_id=target,
            device_id_type=MESH,
        )

    def m_all(d, h):
        res = []
        for way in range(2):
            target = dev_f(h, 1 if way == 0 else 3)
            res.append(m_copy(d, 2 * way, s1.at[d, way], r1.at[d, way], target))
            res.append(m_copy(d, 2 * way + 1, s1s.at[d, way], r1s.at[d, way], target))
        for way in range(2):
            target = dev_f(h, 1 if way == 0 else 3)
            res.append(m_copy(d, 4 + 2 * way, s2.at[d, way], r2.at[d, way], target))
            res.append(m_copy(d, 5 + 2 * way, s2s.at[d, way], r2s.at[d, way], target))
        for ds in range(1, RING):
            target = dev_f(1 - h, ds)
            res.append(m_copy(d, 6 + 2 * ds, s3.at[d, ds - 1], r3.at[d, ds - 1], target))
            res.append(m_copy(d, 7 + 2 * ds, s3s.at[d, ds - 1], r3s.at[d, ds - 1], target))
        return res

    m = [m_all(d, d % 2) for d in range(ROWS)]

    def far_part(d):
        h = d % 2
        f, _ = pos(h)
        f2 = lax.rem(f + 2, RING)
        for way in range(2):

            @pl.loop(0, 4, unroll=UNROLL)
            def _(i):
                v = acc[held_tile(d, f2, way * 2 + i // 2, lax.rem(i, 2))]
                coded, scale = encode(v)
                s1[d, way, i] = coded
                s1s[d, way, pl.ds(i, 1), :] = scale

            m[d][2 * way].start()
            m[d][2 * way + 1].start()

    def near_part(d):
        h = d % 2
        f, _ = pos(h)
        for way in range(2):
            fd = lax.rem(f + (1 if way == 0 else 3), RING)
            m[d][2 * way].wait_recv()
            m[d][2 * way + 1].wait_recv()

            @pl.loop(0, 4, unroll=UNROLL)
            def _(i):
                v = acc[held_tile(d, fd, (1 - way) * 2 + i // 2, lax.rem(i, 2))]
                coded, scale = encode(v)
                s2[d, way, (1 - way) * 4 + i] = coded
                s2s[d, way, pl.ds((1 - way) * 4 + i, 1), :] = scale

            @pl.loop(0, 4, unroll=UNROLL)
            def _(i):
                v = acc[held_tile(d, fd, way * 2 + i // 2, lax.rem(i, 2))]
                v = v + decode(r1[d, way, i], r1s[d, way, pl.ds(i, 1), :])
                coded, scale = encode(v)
                s2[d, way, way * 4 + i] = coded
                s2s[d, way, pl.ds(way * 4 + i, 1), :] = scale

            m[d][4 + 2 * way].start()
            m[d][5 + 2 * way].start()

    def second(d):
        h = d % 2
        f, s = pos(h)
        for kind in range(4, 8):
            m[d][kind].wait_recv()
        for ds in (1, 2, 3, 0):
            s_at = lax.rem(s + ds, RING)

            @pl.loop(0, 2, unroll=2)
            def _(cc):
                where = held_tile(d, f, s_at, cc)
                i = s_at * 2 + cc
                v = (
                    acc[where]
                    + decode(r2[d, 0, i], r2s[d, 0, pl.ds(i, 1), :])
                    + decode(r2[d, 1, i], r2s[d, 1, pl.ds(i, 1), :])
                )
                if ds == 0:
                    fin[d, cc] = v
                else:
                    coded, scale = encode(v)
                    s3[d, ds - 1, cc] = coded
                    s3s[d, ds - 1, pl.ds(cc, 1), :] = scale

            if ds:
                m[d][6 + 2 * ds].start()
                m[d][7 + 2 * ds].start()

    y_copies = []
    for d, (dy, dc) in enumerate(DEST):
        if dy or dc:
            y_copies.append(
                pltpu.make_async_remote_copy(
                    src_ref=fin.at[d],
                    dst_ref=out.at[row],
                    send_sem=y_send.at[d],
                    recv_sem=y_recv.at[d],
                    device_id=dev_row(dy, dc),
                    device_id_type=MESH,
                )
            )
        else:
            y_copies.append(pltpu.make_async_copy(fin.at[d], out.at[row], y_send.at[d]))

    def last(d):
        for kind in range(8, 14):
            m[d][kind].wait_recv()

        @pl.loop(0, 2, unroll=2)
        def _(cc):
            v = fin[d, cc]
            for k in range(3):
                v = v + decode(r3[d, k, cc], r3s[d, k, pl.ds(cc, 1), :])
            fin[d, cc] = v

        y_copies[d].start()

    def both(step, t):
        step(2 * t)
        step(2 * t + 1)

    for u in range(AHEAD):
        first(u)
    tables()
    rows = [taken(at_row(dy, dc)) for dy, dc in DEST]
    relay(0)
    relay(1)
    pass_on(0)
    relay(2)
    pass_on(1)
    a_copy.wait()
    arrived(0)
    for q in range(NCH - 1):
        dense_a(q, rows)
        hooks = [(2, functools.partial(pass_on, 2 * q + 2))]
        hooks.append((1, functools.partial(relay, 2 * q + 3)))
        if 2 * q + 4 < UNITS:
            hooks.append((3, functools.partial(relay, 2 * q + 4)))
        chunk(q, hooks)
        pass_on(2 * q + 3)
        arrived(q + 1)
    dense_a(NCH - 1, rows)

    def ready(t):
        for h in range(2):
            f, _ = pos(h)
            multiply(NCH - 1, h, lax.rem(f + 2, RING), place(2 * t + h), TILE)
            far_part(2 * t + h)
        for h in range(2):
            f, _ = pos(h)

            @pl.loop(0, NSTEP - 1)
            def _(i):
                multiply(NCH - 1, h, lax.rem(f + 3 + i, RING), place(2 * t + h), TILE)

    def sent():
        for copy in w_copies:
            copy.wait_send()
        for u in range(UNITS):
            for copy in copies[u]:
                copy.wait_send()

    def sent_part(t, kinds):
        for d in (2 * t, 2 * t + 1):
            for kind in kinds:
                m[d][kind].wait_send()

    near = functools.partial(both, near_part)
    across = functools.partial(both, second)
    finish = functools.partial(both, last)

    steps = {"F": ready, "N": near, "S": across, "L": finish}
    for step, t in ORDER:
        if step == "L" and t == 0:
            sent()
        if step == "L":
            sent_part(t, range(8))
        steps[step](t)
    for t in range(ROWS // 2):
        sent_part(t, range(8, 14))
    for copy in y_copies:
        copy.wait()


def exchange(row_perm, a_cols, b_cols, a_vals, b_vals):
    bf16, f32, i16, i32 = jnp.bfloat16, jnp.float32, jnp.int16, jnp.int32
    t2 = (TILE, TILE)
    b_chunk = pltpu.VMEM((ROWS * PIECE + 1, *t2), bf16)
    dma = pltpu.SemaphoreType.DMA
    return pl.pallas_call(
        kernel,
        out_shape=jax.ShapeDtypeStruct((ROWS, 2, *t2), f32),
        in_specs=[
            pl.BlockSpec(memory_space=pltpu.SMEM),
            pl.BlockSpec(memory_space=pltpu.VMEM),
            pl.BlockSpec(memory_space=pltpu.VMEM),
            pl.BlockSpec(memory_space=pl.ANY),
            pl.BlockSpec(memory_space=pl.ANY),
        ],
        out_specs=pl.BlockSpec(memory_space=pl.ANY),
        scratch_shapes=[
            pltpu.VMEM((ROWS * KA + 1, *t2), bf16),
            b_chunk, b_chunk, b_chunk, b_chunk, b_chunk, b_chunk,
            pltpu.VMEM((ROWS * TILE, CHUNK * TILE), bf16),
            pltpu.VMEM((ROWS * TILE, NC * TILE), f32),
            pltpu.VMEM((ROWS, TILE), i32),
            pltpu.VMEM((ROWS, TILE), i32),
            pltpu.VMEM((NC, TILE), i32),
            pltpu.VMEM((NC, TILE), i32),
            pltpu.VMEM((ROWS, NC, TILE), i32),
            pltpu.SMEM((ROWS, TILE), i32),
            pltpu.SMEM((NC, TILE), i32),
            pltpu.VMEM((ROWS, 2, 4, *t2), i16),
            pltpu.VMEM((ROWS, 2, 8, TILE), f32),
            pltpu.VMEM((ROWS, 2, 4, *t2), i16),
            pltpu.VMEM((ROWS, 2, 8, TILE), f32),
            pltpu.VMEM((ROWS, 2, 8, *t2), i16),
            pltpu.VMEM((ROWS, 2, 8, TILE), f32),
            pltpu.VMEM((ROWS, 2, 8, *t2), i16),
            pltpu.VMEM((ROWS, 2, 8, TILE), f32),
            pltpu.VMEM((ROWS, 3, 2, *t2), i16),
            pltpu.VMEM((ROWS, 3, 8, TILE), f32),
            pltpu.VMEM((ROWS, 3, 2, *t2), i16),
            pltpu.VMEM((ROWS, 3, 8, TILE), f32),
            pltpu.VMEM((ROWS, 2, *t2), f32),
            dma((UNITS, 9)), dma((UNITS, 9)), dma((NCH + 3,)), dma((ROWS,)), dma((ROWS,)),
            dma((ROWS, 14)), dma((ROWS, 14)), dma((ROWS,)), dma((ROWS,)),
        ],
        compiler_params=pltpu.CompilerParams(
            collective_id=0, has_side_effects=True, vmem_limit_bytes=60 * 1024 * 1024
        ),
        name="exchange",
    )(row_perm, a_cols, b_cols, a_vals, b_vals)


def on_device(a_vals, a_cols, b_vals, b_cols, row_perm):
    got = exchange(
        row_perm,
        a_cols.reshape(ROWS, KA),
        b_cols.T,
        a_vals.reshape(ROWS * KA, TILE, TILE),
        b_vals.reshape(KWR * 2, TILE, TILE),
    )
    own_row = lax.axis_index("row")
    source = lax.dynamic_slice_in_dim(row_perm, own_row * ROWS, ROWS) // ROWS
    return got.at[source].get(mode="promise_in_bounds")


def solution(mesh):
    placed = (
        P("row", ("col", "layer"), None, None, None),
        P("row", ("col", "layer"), None),
        P(("col", "layer"), "row", None, None),
        P(("col", "layer"), "row"),
        P(),
    )
    return jax.shard_map(
        on_device,
        mesh=mesh,
        in_specs=placed,
        out_specs=P("row", ("col", "layer"), None, None),
        check_vma=False,
    )
```

```python
import functools

import jax
import jax.numpy as jnp
from jax import lax
from jax.experimental import pallas as pl
from jax.experimental.pallas import tpu as pltpu
from jax.sharding import PartitionSpec as P

TILE = 128
NC = 32
KWR = 24
KA = 12
ROWS = 8
RING = 4
CHUNK = 4
NCH = KWR // CHUNK
PIECE = CHUNK * 2
UNITS = NCH * 2
UNIT = PIECE // 2
HALF = UNIT // 2
AHEAD = 2
MINOR = ROWS // 2 * TILE
NB = 1024
NSTEP = NC * TILE // NB
TOP = 32767.0
UNROLL = 4
DEST = ((2, 0), (2, 1), (1, 0), (3, 0), (1, 1), (3, 1), (0, 0), (0, 1))
MESH = pl.DeviceIdType.MESH
ORDER = (
    ("F", 0), ("F", 1), ("N", 0), ("F", 2), ("N", 1), ("F", 3), ("N", 2), ("S", 0),
    ("N", 3), ("S", 1), ("L", 0), ("S", 2), ("L", 1), ("S", 3), ("L", 2), ("L", 3),
)


def encode(v):
    top = jnp.maximum(jnp.max(jnp.abs(v), axis=0, keepdims=True), 1e-30)
    coded = jnp.round(v * (TOP / top)).astype(jnp.int32).astype(jnp.int16)
    return coded, top * (1.0 / TOP)


def decode(coded, scale):
    return coded.astype(jnp.int32).astype(jnp.float32) * scale


def kernel(
    perm, ac_ref, bc_ref, a_hbm, b_hbm, out,
    a_v, b_v0, b_v1, b_v2, b_v3, b_v4, b_v5, ad, acc, ia_v, bc_v, ib_v, w_own, w_all, ia, ib,
    s1, s1s, r1, r1s, s2, s2s, r2, r2s, s3, s3s, r3, r3s, fin,
    g_send, g_recv, loc_sem, w_send, w_recv, m_send, m_recv, y_send, y_recv,
):
    b_v = (b_v0, b_v1, b_v2, b_v3, b_v4, b_v5)
    row = lax.axis_index("row")
    x = lax.axis_index("col")
    z = lax.axis_index("layer")
    y, c = row // 2, lax.rem(row, 2)

    def at_row(dy, dc):
        return lax.rem(y + dy, RING) * 2 + lax.rem(c + dc, 2)

    def dev_row(dy, dc):
        return (at_row(dy, dc), x, z)

    def dev_f(h, df):
        if h == 0:
            return (row, lax.rem(x + df, RING), z)
        return (row, x, lax.rem(z + df, RING))

    barrier = pltpu.get_barrier_semaphore()
    peers = [dev_row(dy, dc) for dy in range(RING) for dc in range(2) if dy or dc]
    peers += [dev_f(h, df) for h in range(2) for df in range(1, RING)]
    for peer in peers:
        pl.semaphore_signal(barrier, inc=1, device_id=peer, device_id_type=MESH)

    lane = lax.broadcasted_iota(jnp.int32, (ROWS, TILE), 1)
    left = lax.broadcasted_iota(jnp.int32, (ROWS, TILE), 0)
    table = jnp.full((ROWS, TILE), ROWS * KA, jnp.int32)
    for k in range(KA):
        table = jnp.where(ac_ref[:, k : k + 1] == lane, left * KA + k, table)
    ia_v[...] = table
    ia_copy = pltpu.make_async_copy(ia_v, ia, loc_sem.at[NCH + 1])
    ia_copy.start()
    bc_v[...] = jnp.full((ROWS, TILE), -1, jnp.int32)
    bc_v[0:2, 0:KWR] = bc_ref[...]
    col = lax.broadcasted_iota(jnp.int32, (NC, TILE), 0)
    inner = lax.rem(lax.broadcasted_iota(jnp.int32, (NC, TILE), 1), CHUNK)
    table = jnp.zeros((NC, TILE), jnp.int32)
    for k in range(2):
        table = jnp.where(bc_v[k : k + 1, :] == col, row * PIECE + inner * 2 + k + 1, table)
    w_own[...] = table

    a_copy = pltpu.make_async_copy(a_hbm, a_v.at[pl.ds(0, ROWS * KA)], loc_sem.at[NCH])
    a_copy.start()
    own = [
        pltpu.make_async_copy(
            b_hbm.at[pl.ds(q * PIECE, PIECE)], b_v[q].at[pl.ds(row * PIECE, PIECE)], loc_sem.at[q]
        )
        for q in range(NCH)
    ]
    for q in range(NCH):
        own[q].start()
    zero = jnp.zeros((TILE, TILE), jnp.bfloat16)
    a_v[ROWS * KA] = zero
    for q in range(NCH):
        b_v[q][ROWS * PIECE] = zero
    pl.semaphore_wait(barrier, len(peers))

    w_copies = [
        pltpu.make_async_remote_copy(
            src_ref=w_own,
            dst_ref=w_all.at[row],
            send_sem=w_send.at[2 * dy + dc],
            recv_sem=w_recv.at[2 * dy + dc],
            device_id=dev_row(dy, dc),
            device_id_type=MESH,
        )
        for dy in range(RING)
        for dc in range(2)
        if dy or dc
    ]
    for copy in w_copies:
        copy.start()

    def tables():
        w_all[row] = w_own[...]
        for copy in w_copies:
            copy.wait_recv()
        top = w_all[0]
        for source in range(1, ROWS):
            top = jnp.maximum(top, w_all[source])
        ib_v[...] = jnp.where(top > 0, top - 1, ROWS * PIECE)
        ib_copy = pltpu.make_async_copy(ib_v, ib, loc_sem.at[NCH + 2])
        ib_copy.start()
        ib_copy.wait()
        ia_copy.wait()

    def g_copy(u, kind, src, dst_at, n, target):
        return pltpu.make_async_remote_copy(
            src_ref=src,
            dst_ref=b_v[u // 2].at[pl.ds(dst_at, n)],
            send_sem=g_send.at[u, kind],
            recv_sem=g_recv.at[u, kind],
            device_id=target,
            device_id_type=MESH,
        )

    up, down, sib = dev_row(1, 0), dev_row(3, 0), dev_row(0, 1)

    def g_all(u):
        at_own, at_below, at_above, at_far = (
            at_row(d, 0) * PIECE + u % 2 * UNIT for d in (0, 3, 1, 2)
        )
        mine = b_hbm.at[pl.ds(u * UNIT, UNIT)]
        held = lambda at, n: b_v[u // 2].at[pl.ds(at, n)]
        return (
            g_copy(u, 0, mine, at_own, UNIT, up),
            g_copy(u, 1, mine, at_own, UNIT, down),
            g_copy(u, 2, mine, at_own, UNIT, sib),
            g_copy(u, 3, held(at_below, HALF), at_below, HALF, up),
            g_copy(u, 4, held(at_above + HALF, HALF), at_above + HALF, HALF, down),
            g_copy(u, 5, held(at_below, UNIT), at_below, UNIT, sib),
            g_copy(u, 6, held(at_above, UNIT), at_above, UNIT, sib),
            g_copy(u, 7, held(at_far, HALF), at_far, HALF, sib),
            g_copy(u, 8, held(at_far + HALF, HALF), at_far + HALF, HALF, sib),
        )

    copies = [g_all(u) for u in range(UNITS)]

    def first(u):
        for kind in (0, 1, 2):
            copies[u][kind].start()

    def relay(u):
        copies[u][0].wait_recv()
        copies[u][3].start()
        copies[u][5].start()
        copies[u][1].wait_recv()
        copies[u][4].start()
        copies[u][6].start()
        if u + AHEAD < UNITS:
            first(u + AHEAD)

    def pass_on(u):
        copies[u][3].wait_recv()
        copies[u][7].start()
        copies[u][4].wait_recv()
        copies[u][8].start()

    def arrived(q):
        own[q].wait()
        for u in (2 * q, 2 * q + 1):
            for kind in (2, 5, 6, 7, 8):
                copies[u][kind].wait_recv()

    def taken(j):
        total = jnp.int32(0)
        for i in range(ROWS):
            p = perm[j * ROWS + i]
            total = jnp.maximum(total, jnp.where(lax.div(p, ROWS) == row, lax.rem(p, ROWS), 0))
        return total

    def place(d):
        return d % 2 * MINOR + d // 2 * TILE

    def dense_a(q, rows):
        for d in range(ROWS):
            for k in range(CHUNK):
                ad[place(d) : place(d) + TILE, k * TILE : (k + 1) * TILE] = a_v[
                    ia[rows[d], q * CHUNK + k]
                ]

    def multiply(q, h, n, r0, count):
        def tile(k, i):
            col = n * 8 + i if h == 0 else (i // 2 * RING + n) * 2 + i % 2
            return b_v[q][ib[col, q * CHUNK + k]]

        right = jnp.concatenate(
            [jnp.concatenate([tile(k, i) for i in range(8)], axis=1) for k in range(CHUNK)], axis=0
        )
        cols = pl.ds(pl.multiple_of(n * NB, NB), NB)
        part = jnp.dot(ad[r0 : r0 + count, :], right, preferred_element_type=jnp.float32)
        if q == 0:
            acc[r0 : r0 + count, cols] = part
        else:
            acc[r0 : r0 + count, cols] = acc[r0 : r0 + count, cols] + part

    def chunk(q, hooks):
        @pl.loop(0, NSTEP)
        def _(n):
            for step, act in hooks:
                pl.when(n == step)(act)
            for h in range(2):
                multiply(q, h, n, h * MINOR, MINOR)

    def pos(h):
        return (x, z) if h == 0 else (z, x)

    def held_tile(d, f_at, s_at, cc):
        lanes = pl.ds(pl.multiple_of((f_at * RING + s_at) * 2 * TILE + cc * TILE, TILE), TILE)
        return (slice(place(d), place(d) + TILE), lanes)

    def m_copy(d, kind, src, dst, target):
        return pltpu.make_async_remote_copy(
            src_ref=src,
            dst_ref=dst,
            send_sem=m_send.at[d, kind],
            recv_sem=m_recv.at[d, kind],
            device_id=target,
            device_id_type=MESH,
        )

    def m_all(d, h):
        res = []
        for way in range(2):
            target = dev_f(h, 1 if way == 0 else 3)
            res.append(m_copy(d, 2 * way, s1.at[d, way], r1.at[d, way], target))
            res.append(m_copy(d, 2 * way + 1, s1s.at[d, way], r1s.at[d, way], target))
        for way in range(2):
            target = dev_f(h, 1 if way == 0 else 3)
            res.append(m_copy(d, 4 + 2 * way, s2.at[d, way], r2.at[d, way], target))
            res.append(m_copy(d, 5 + 2 * way, s2s.at[d, way], r2s.at[d, way], target))
        for ds in range(1, RING):
            target = dev_f(1 - h, ds)
            res.append(m_copy(d, 6 + 2 * ds, s3.at[d, ds - 1], r3.at[d, ds - 1], target))
            res.append(m_copy(d, 7 + 2 * ds, s3s.at[d, ds - 1], r3s.at[d, ds - 1], target))
        return res

    m = [m_all(d, d % 2) for d in range(ROWS)]

    def far_part(d):
        h = d % 2
        f, _ = pos(h)
        f2 = lax.rem(f + 2, RING)
        for way in range(2):

            @pl.loop(0, 4, unroll=UNROLL)
            def _(i):
                v = acc[held_tile(d, f2, way * 2 + i // 2, lax.rem(i, 2))]
                coded, scale = encode(v)
                s1[d, way, i] = coded
                s1s[d, way, pl.ds(i, 1), :] = scale

            m[d][2 * way].start()
            m[d][2 * way + 1].start()

    def near_part(d):
        h = d % 2
        f, _ = pos(h)
        for way in range(2):
            fd = lax.rem(f + (1 if way == 0 else 3), RING)
            m[d][2 * way].wait_recv()
            m[d][2 * way + 1].wait_recv()

            @pl.loop(0, 4, unroll=UNROLL)
            def _(i):
                v = acc[held_tile(d, fd, (1 - way) * 2 + i // 2, lax.rem(i, 2))]
                coded, scale = encode(v)
                s2[d, way, (1 - way) * 4 + i] = coded
                s2s[d, way, pl.ds((1 - way) * 4 + i, 1), :] = scale

            @pl.loop(0, 4, unroll=UNROLL)
            def _(i):
                v = acc[held_tile(d, fd, way * 2 + i // 2, lax.rem(i, 2))]
                v = v + decode(r1[d, way, i], r1s[d, way, pl.ds(i, 1), :])
                coded, scale = encode(v)
                s2[d, way, way * 4 + i] = coded
                s2s[d, way, pl.ds(way * 4 + i, 1), :] = scale

            m[d][4 + 2 * way].start()
            m[d][5 + 2 * way].start()

    def second(d):
        h = d % 2
        f, s = pos(h)
        for kind in range(4, 8):
            m[d][kind].wait_recv()
        for ds in (1, 2, 3, 0):
            s_at = lax.rem(s + ds, RING)

            @pl.loop(0, 2, unroll=2)
            def _(cc):
                where = held_tile(d, f, s_at, cc)
                i = s_at * 2 + cc
                v = (
                    acc[where]
                    + decode(r2[d, 0, i], r2s[d, 0, pl.ds(i, 1), :])
                    + decode(r2[d, 1, i], r2s[d, 1, pl.ds(i, 1), :])
                )
                if ds == 0:
                    fin[d, cc] = v
                else:
                    coded, scale = encode(v)
                    s3[d, ds - 1, cc] = coded
                    s3s[d, ds - 1, pl.ds(cc, 1), :] = scale

            if ds:
                m[d][6 + 2 * ds].start()
                m[d][7 + 2 * ds].start()

    y_copies = []
    for d, (dy, dc) in enumerate(DEST):
        if dy or dc:
            y_copies.append(
                pltpu.make_async_remote_copy(
                    src_ref=fin.at[d],
                    dst_ref=out.at[row],
                    send_sem=y_send.at[d],
                    recv_sem=y_recv.at[d],
                    device_id=dev_row(dy, dc),
                    device_id_type=MESH,
                )
            )
        else:
            y_copies.append(pltpu.make_async_copy(fin.at[d], out.at[row], y_send.at[d]))

    def last(d):
        for kind in range(8, 14):
            m[d][kind].wait_recv()

        @pl.loop(0, 2, unroll=2)
        def _(cc):
            v = fin[d, cc]
            for k in range(3):
                v = v + decode(r3[d, k, cc], r3s[d, k, pl.ds(cc, 1), :])
            fin[d, cc] = v

        y_copies[d].start()

    def both(step, t):
        step(2 * t)
        step(2 * t + 1)

    for u in range(AHEAD):
        first(u)
    tables()
    rows = [taken(at_row(dy, dc)) for dy, dc in DEST]
    relay(0)
    relay(1)
    pass_on(0)
    relay(2)
    pass_on(1)
    a_copy.wait()
    dense_a(0, rows)
    arrived(0)
    for q in range(NCH - 1):
        hooks = [(2, functools.partial(pass_on, 2 * q + 2))]
        hooks.append((1, functools.partial(relay, 2 * q + 3)))
        if 2 * q + 4 < UNITS:
            hooks.append((3, functools.partial(relay, 2 * q + 4)))
        chunk(q, hooks)
        dense_a(q + 1, rows)
        pass_on(2 * q + 3)
        arrived(q + 1)

    def ready(t):
        for h in range(2):
            f, _ = pos(h)
            multiply(NCH - 1, h, lax.rem(f + 2, RING), place(2 * t + h), TILE)
            far_part(2 * t + h)
        for h in range(2):
            f, _ = pos(h)

            @pl.loop(0, NSTEP - 1)
            def _(i):
                multiply(NCH - 1, h, lax.rem(f + 3 + i, RING), place(2 * t + h), TILE)

    def sent():
        for copy in w_copies:
            copy.wait_send()
        for u in range(UNITS):
            for copy in copies[u]:
                copy.wait_send()

    def sent_part(t, kinds):
        for d in (2 * t, 2 * t + 1):
            for kind in kinds:
                m[d][kind].wait_send()

    near = functools.partial(both, near_part)
    across = functools.partial(both, second)
    finish = functools.partial(both, last)

    steps = {"F": ready, "N": near, "S": across, "L": finish}
    for step, t in ORDER:
        if step == "L" and t == 0:
            sent()
        if step == "L":
            sent_part(t, range(8))
        steps[step](t)
    for t in range(ROWS // 2):
        sent_part(t, range(8, 14))
    for copy in y_copies:
        copy.wait()


def exchange(row_perm, a_cols, b_cols, a_vals, b_vals):
    bf16, f32, i16, i32 = jnp.bfloat16, jnp.float32, jnp.int16, jnp.int32
    t2 = (TILE, TILE)
    b_chunk = pltpu.VMEM((ROWS * PIECE + 1, *t2), bf16)
    dma = pltpu.SemaphoreType.DMA
    return pl.pallas_call(
        kernel,
        out_shape=jax.ShapeDtypeStruct((ROWS, 2, *t2), f32),
        in_specs=[
            pl.BlockSpec(memory_space=pltpu.SMEM),
            pl.BlockSpec(memory_space=pltpu.VMEM),
            pl.BlockSpec(memory_space=pltpu.VMEM),
            pl.BlockSpec(memory_space=pl.ANY),
            pl.BlockSpec(memory_space=pl.ANY),
        ],
        out_specs=pl.BlockSpec(memory_space=pl.ANY),
        scratch_shapes=[
            pltpu.VMEM((ROWS * KA + 1, *t2), bf16),
            b_chunk, b_chunk, b_chunk, b_chunk, b_chunk, b_chunk,
            pltpu.VMEM((ROWS * TILE, CHUNK * TILE), bf16),
            pltpu.VMEM((ROWS * TILE, NC * TILE), f32),
            pltpu.VMEM((ROWS, TILE), i32),
            pltpu.VMEM((ROWS, TILE), i32),
            pltpu.VMEM((NC, TILE), i32),
            pltpu.VMEM((NC, TILE), i32),
            pltpu.VMEM((ROWS, NC, TILE), i32),
            pltpu.SMEM((ROWS, TILE), i32),
            pltpu.SMEM((NC, TILE), i32),
            pltpu.VMEM((ROWS, 2, 4, *t2), i16),
            pltpu.VMEM((ROWS, 2, 8, TILE), f32),
            pltpu.VMEM((ROWS, 2, 4, *t2), i16),
            pltpu.VMEM((ROWS, 2, 8, TILE), f32),
            pltpu.VMEM((ROWS, 2, 8, *t2), i16),
            pltpu.VMEM((ROWS, 2, 8, TILE), f32),
            pltpu.VMEM((ROWS, 2, 8, *t2), i16),
            pltpu.VMEM((ROWS, 2, 8, TILE), f32),
            pltpu.VMEM((ROWS, 3, 2, *t2), i16),
            pltpu.VMEM((ROWS, 3, 8, TILE), f32),
            pltpu.VMEM((ROWS, 3, 2, *t2), i16),
            pltpu.VMEM((ROWS, 3, 8, TILE), f32),
            pltpu.VMEM((ROWS, 2, *t2), f32),
            dma((UNITS, 9)), dma((UNITS, 9)), dma((NCH + 3,)), dma((ROWS,)), dma((ROWS,)),
            dma((ROWS, 14)), dma((ROWS, 14)), dma((ROWS,)), dma((ROWS,)),
        ],
        compiler_params=pltpu.CompilerParams(
            collective_id=0, has_side_effects=True, vmem_limit_bytes=60 * 1024 * 1024
        ),
        name="exchange",
    )(row_perm, a_cols, b_cols, a_vals, b_vals)


def on_device(a_vals, a_cols, b_vals, b_cols, row_perm):
    got = exchange(
        row_perm,
        a_cols.reshape(ROWS, KA),
        b_cols.T,
        a_vals.reshape(ROWS * KA, TILE, TILE),
        b_vals.reshape(KWR * 2, TILE, TILE),
    )
    own_row = lax.axis_index("row")
    source = lax.dynamic_slice_in_dim(row_perm, own_row * ROWS, ROWS) // ROWS
    return got.at[source].get(mode="promise_in_bounds")


def solution(mesh):
    placed = (
        P("row", ("col", "layer"), None, None, None),
        P("row", ("col", "layer"), None),
        P(("col", "layer"), "row", None, None),
        P(("col", "layer"), "row"),
        P(),
    )
    return jax.shard_map(
        on_device,
        mesh=mesh,
        in_specs=placed,
        out_specs=P("row", ("col", "layer"), None, None),
        check_vma=False,
    )
```

```python
import functools

import jax
import jax.numpy as jnp
from jax import lax
from jax.experimental import pallas as pl
from jax.experimental.pallas import tpu as pltpu
from jax.sharding import PartitionSpec as P

TILE = 128
NC = 32
KWR = 24
KA = 12
ROWS = 8
RING = 4
CHUNK = 4
NCH = KWR // CHUNK
PIECE = CHUNK * 2
UNITS = NCH * 2
UNIT = PIECE // 2
HALF = UNIT // 2
AHEAD = 2
MINOR = ROWS // 2 * TILE
NB = 1024
NSTEP = NC * TILE // NB
TOP = 32767.0
UNROLL = 4
DEST = ((2, 0), (2, 1), (1, 0), (3, 0), (1, 1), (3, 1), (0, 0), (0, 1))
MESH = pl.DeviceIdType.MESH
ORDER = (
    ("F", 0), ("F", 1), ("N", 0), ("F", 2), ("N", 1), ("F", 3), ("N", 2), ("S", 0),
    ("N", 3), ("S", 1), ("L", 0), ("S", 2), ("L", 1), ("S", 3), ("L", 2), ("L", 3),
)


def encode(v):
    top = jnp.maximum(jnp.max(jnp.abs(v), axis=0, keepdims=True), 1e-30)
    coded = jnp.round(v * (TOP / top)).astype(jnp.int32).astype(jnp.int16)
    return coded, top * (1.0 / TOP)


def decode(coded, scale):
    return coded.astype(jnp.int32).astype(jnp.float32) * scale


def kernel(
    perm, ac_ref, bc_ref, a_hbm, b_hbm, out,
    a_v, b_v0, b_v1, b_v2, b_v3, b_v4, b_v5, ad, acc, ia_v, bc_v, ib_v, w_own, w_all, ia, ib,
    s1, s1s, r1, r1s, s2, s2s, r2, r2s, s3, s3s, r3, r3s, fin,
    g_send, g_recv, loc_sem, w_send, w_recv, m_send, m_recv, y_send, y_recv,
):
    b_v = (b_v0, b_v1, b_v2, b_v3, b_v4, b_v5)
    row = lax.axis_index("row")
    x = lax.axis_index("col")
    z = lax.axis_index("layer")
    y, c = row // 2, lax.rem(row, 2)

    def at_row(dy, dc):
        return lax.rem(y + dy, RING) * 2 + lax.rem(c + dc, 2)

    def dev_row(dy, dc):
        return (at_row(dy, dc), x, z)

    def dev_f(h, df):
        if h == 0:
            return (row, lax.rem(x + df, RING), z)
        return (row, x, lax.rem(z + df, RING))

    barrier = pltpu.get_barrier_semaphore()
    peers = [dev_row(dy, dc) for dy in range(RING) for dc in range(2) if dy or dc]
    peers += [dev_f(h, df) for h in range(2) for df in range(1, RING)]
    for peer in peers:
        pl.semaphore_signal(barrier, inc=1, device_id=peer, device_id_type=MESH)

    lane = lax.broadcasted_iota(jnp.int32, (ROWS, TILE), 1)
    left = lax.broadcasted_iota(jnp.int32, (ROWS, TILE), 0)
    table = jnp.full((ROWS, TILE), ROWS * KA, jnp.int32)
    for k in range(KA):
        table = jnp.where(ac_ref[:, k : k + 1] == lane, left * KA + k, table)
    ia_v[...] = table
    ia_copy = pltpu.make_async_copy(ia_v, ia, loc_sem.at[NCH + 1])
    ia_copy.start()
    bc_v[...] = jnp.full((ROWS, TILE), -1, jnp.int32)
    bc_v[0:2, 0:KWR] = bc_ref[...]
    col = lax.broadcasted_iota(jnp.int32, (NC, TILE), 0)
    inner = lax.rem(lax.broadcasted_iota(jnp.int32, (NC, TILE), 1), CHUNK)
    table = jnp.zeros((NC, TILE), jnp.int32)
    for k in range(2):
        table = jnp.where(bc_v[k : k + 1, :] == col, row * PIECE + inner * 2 + k + 1, table)
    w_own[...] = table

    a_copy = pltpu.make_async_copy(a_hbm, a_v.at[pl.ds(0, ROWS * KA)], loc_sem.at[NCH])
    a_copy.start()
    own = [
        pltpu.make_async_copy(
            b_hbm.at[pl.ds(q * PIECE, PIECE)], b_v[q].at[pl.ds(row * PIECE, PIECE)], loc_sem.at[q]
        )
        for q in range(NCH)
    ]
    for q in range(NCH):
        own[q].start()
    zero = jnp.zeros((TILE, TILE), jnp.bfloat16)
    a_v[ROWS * KA] = zero
    for q in range(NCH):
        b_v[q][ROWS * PIECE] = zero
    pl.semaphore_wait(barrier, len(peers))

    w_copies = [
        pltpu.make_async_remote_copy(
            src_ref=w_own,
            dst_ref=w_all.at[row],
            send_sem=w_send.at[2 * dy + dc],
            recv_sem=w_recv.at[2 * dy + dc],
            device_id=dev_row(dy, dc),
            device_id_type=MESH,
        )
        for dy in range(RING)
        for dc in range(2)
        if dy or dc
    ]
    for copy in w_copies:
        copy.start()

    def tables():
        w_all[row] = w_own[...]
        for copy in w_copies:
            copy.wait_recv()
        top = w_all[0]
        for source in range(1, ROWS):
            top = jnp.maximum(top, w_all[source])
        ib_v[...] = jnp.where(top > 0, top - 1, ROWS * PIECE)
        ib_copy = pltpu.make_async_copy(ib_v, ib, loc_sem.at[NCH + 2])
        ib_copy.start()
        ib_copy.wait()
        ia_copy.wait()

    def g_copy(u, kind, src, dst_at, n, target):
        return pltpu.make_async_remote_copy(
            src_ref=src,
            dst_ref=b_v[u // 2].at[pl.ds(dst_at, n)],
            send_sem=g_send.at[u, kind],
            recv_sem=g_recv.at[u, kind],
            device_id=target,
            device_id_type=MESH,
        )

    up, down, sib = dev_row(1, 0), dev_row(3, 0), dev_row(0, 1)

    def g_all(u):
        at_own, at_below, at_above, at_far = (
            at_row(d, 0) * PIECE + u % 2 * UNIT for d in (0, 3, 1, 2)
        )
        mine = b_hbm.at[pl.ds(u * UNIT, UNIT)]
        held = lambda at, n: b_v[u // 2].at[pl.ds(at, n)]
        return (
            g_copy(u, 0, mine, at_own, UNIT, up),
            g_copy(u, 1, mine, at_own, UNIT, down),
            g_copy(u, 2, mine, at_own, UNIT, sib),
            g_copy(u, 3, held(at_below, HALF), at_below, HALF, up),
            g_copy(u, 4, held(at_above + HALF, HALF), at_above + HALF, HALF, down),
            g_copy(u, 5, held(at_below, UNIT), at_below, UNIT, sib),
            g_copy(u, 6, held(at_above, UNIT), at_above, UNIT, sib),
            g_copy(u, 7, held(at_far, HALF), at_far, HALF, sib),
            g_copy(u, 8, held(at_far + HALF, HALF), at_far + HALF, HALF, sib),
        )

    copies = [g_all(u) for u in range(UNITS)]

    def first(u):
        for kind in (0, 1, 2):
            copies[u][kind].start()

    def relay(u):
        copies[u][0].wait_recv()
        copies[u][3].start()
        copies[u][5].start()
        copies[u][1].wait_recv()
        copies[u][4].start()
        copies[u][6].start()
        if u + AHEAD < UNITS:
            first(u + AHEAD)

    def pass_on(u):
        copies[u][3].wait_recv()
        copies[u][7].start()
        copies[u][4].wait_recv()
        copies[u][8].start()

    def arrived(q):
        own[q].wait()
        for u in (2 * q, 2 * q + 1):
            for kind in (2, 5, 6, 7, 8):
                copies[u][kind].wait_recv()

    def taken(j):
        total = jnp.int32(0)
        for i in range(ROWS):
            p = perm[j * ROWS + i]
            total = jnp.maximum(total, jnp.where(lax.div(p, ROWS) == row, lax.rem(p, ROWS), 0))
        return total

    def place(d):
        return d % 2 * MINOR + d // 2 * TILE

    def dense_a(q, rows):
        for d in range(ROWS):
            for k in range(CHUNK):
                ad[place(d) : place(d) + TILE, k * TILE : (k + 1) * TILE] = a_v[
                    ia[rows[d], q * CHUNK + k]
                ]

    def multiply(q, h, n, r0, count):
        def tile(k, i):
            col = n * 8 + i if h == 0 else (i // 2 * RING + n) * 2 + i % 2
            return b_v[q][ib[col, q * CHUNK + k]]

        right = jnp.concatenate(
            [jnp.concatenate([tile(k, i) for i in range(8)], axis=1) for k in range(CHUNK)], axis=0
        )
        cols = pl.ds(pl.multiple_of(n * NB, NB), NB)
        part = jnp.dot(ad[r0 : r0 + count, :], right, preferred_element_type=jnp.float32)
        if q == 0:
            acc[r0 : r0 + count, cols] = part
        else:
            acc[r0 : r0 + count, cols] = acc[r0 : r0 + count, cols] + part

    def chunk(q, hooks):
        @pl.loop(0, NSTEP)
        def _(n):
            for step, act in hooks:
                pl.when(n == step)(act)
            for h in range(2):
                multiply(q, h, n, h * MINOR, MINOR)

    def pos(h):
        return (x, z) if h == 0 else (z, x)

    def held_tile(d, f_at, s_at, cc):
        lanes = pl.ds(pl.multiple_of((f_at * RING + s_at) * 2 * TILE + cc * TILE, TILE), TILE)
        return (slice(place(d), place(d) + TILE), lanes)

    def m_copy(d, kind, src, dst, target):
        return pltpu.make_async_remote_copy(
            src_ref=src,
            dst_ref=dst,
            send_sem=m_send.at[d, kind],
            recv_sem=m_recv.at[d, kind],
            device_id=target,
            device_id_type=MESH,
        )

    def m_all(d, h):
        res = []
        for way in range(2):
            target = dev_f(h, 1 if way == 0 else 3)
            res.append(m_copy(d, 2 * way, s1.at[d, way], r1.at[d, way], target))
            res.append(m_copy(d, 2 * way + 1, s1s.at[d, way], r1s.at[d, way], target))
        for way in range(2):
            target = dev_f(h, 1 if way == 0 else 3)
            res.append(m_copy(d, 4 + 2 * way, s2.at[d, way], r2.at[d, way], target))
            res.append(m_copy(d, 5 + 2 * way, s2s.at[d, way], r2s.at[d, way], target))
        for ds in range(1, RING):
            target = dev_f(1 - h, ds)
            res.append(m_copy(d, 6 + 2 * ds, s3.at[d, ds - 1], r3.at[d, ds - 1], target))
            res.append(m_copy(d, 7 + 2 * ds, s3s.at[d, ds - 1], r3s.at[d, ds - 1], target))
        return res

    m = [m_all(d, d % 2) for d in range(ROWS)]

    def far_part(d):
        h = d % 2
        f, _ = pos(h)
        f2 = lax.rem(f + 2, RING)
        for way in range(2):

            @pl.loop(0, 4, unroll=UNROLL)
            def _(i):
                v = acc[held_tile(d, f2, way * 2 + i // 2, lax.rem(i, 2))]
                coded, scale = encode(v)
                s1[d, way, i] = coded
                s1s[d, way, pl.ds(i, 1), :] = scale

            m[d][2 * way].start()
            m[d][2 * way + 1].start()

    def near_part(d):
        h = d % 2
        f, _ = pos(h)
        for way in range(2):
            fd = lax.rem(f + (1 if way == 0 else 3), RING)
            m[d][2 * way].wait_recv()
            m[d][2 * way + 1].wait_recv()

            @pl.loop(0, 4, unroll=UNROLL)
            def _(i):
                v = acc[held_tile(d, fd, (1 - way) * 2 + i // 2, lax.rem(i, 2))]
                coded, scale = encode(v)
                s2[d, way, (1 - way) * 4 + i] = coded
                s2s[d, way, pl.ds((1 - way) * 4 + i, 1), :] = scale

            @pl.loop(0, 4, unroll=UNROLL)
            def _(i):
                v = acc[held_tile(d, fd, way * 2 + i // 2, lax.rem(i, 2))]
                v = v + decode(r1[d, way, i], r1s[d, way, pl.ds(i, 1), :])
                coded, scale = encode(v)
                s2[d, way, way * 4 + i] = coded
                s2s[d, way, pl.ds(way * 4 + i, 1), :] = scale

            m[d][4 + 2 * way].start()
            m[d][5 + 2 * way].start()

    def second(d):
        h = d % 2
        f, s = pos(h)
        for kind in range(4, 8):
            m[d][kind].wait_recv()
        for ds in (1, 2, 3, 0):
            s_at = lax.rem(s + ds, RING)

            @pl.loop(0, 2, unroll=2)
            def _(cc):
                where = held_tile(d, f, s_at, cc)
                i = s_at * 2 + cc
                v = (
                    acc[where]
                    + decode(r2[d, 0, i], r2s[d, 0, pl.ds(i, 1), :])
                    + decode(r2[d, 1, i], r2s[d, 1, pl.ds(i, 1), :])
                )
                if ds == 0:
                    fin[d, cc] = v
                else:
                    coded, scale = encode(v)
                    s3[d, ds - 1, cc] = coded
                    s3s[d, ds - 1, pl.ds(cc, 1), :] = scale

            if ds:
                m[d][6 + 2 * ds].start()
                m[d][7 + 2 * ds].start()

    y_copies = []
    for d, (dy, dc) in enumerate(DEST):
        if dy or dc:
            y_copies.append(
                pltpu.make_async_remote_copy(
                    src_ref=fin.at[d],
                    dst_ref=out.at[row],
                    send_sem=y_send.at[d],
                    recv_sem=y_recv.at[d],
                    device_id=dev_row(dy, dc),
                    device_id_type=MESH,
                )
            )
        else:
            y_copies.append(pltpu.make_async_copy(fin.at[d], out.at[row], y_send.at[d]))

    def last(d):
        for kind in range(8, 14):
            m[d][kind].wait_recv()

        @pl.loop(0, 2, unroll=2)
        def _(cc):
            v = fin[d, cc]
            for k in range(3):
                v = v + decode(r3[d, k, cc], r3s[d, k, pl.ds(cc, 1), :])
            fin[d, cc] = v

        y_copies[d].start()

    def both(step, t):
        step(2 * t)
        step(2 * t + 1)

    for u in range(AHEAD):
        first(u)
    tables()
    rows = [taken(at_row(dy, dc)) for dy, dc in DEST]
    relay(0)
    relay(1)
    pass_on(0)
    relay(2)
    pass_on(1)
    a_copy.wait()
    arrived(0)
    for q in range(NCH - 1):
        dense_a(q, rows)
        hooks = [(2, functools.partial(pass_on, 2 * q + 2))]
        hooks.append((1, functools.partial(relay, 2 * q + 3)))
        if 2 * q + 4 < UNITS:
            hooks.append((3, functools.partial(relay, 2 * q + 4)))
        chunk(q, hooks)
        pass_on(2 * q + 3)
        arrived(q + 1)
    dense_a(NCH - 1, rows)

    def ready(t):
        for h in range(2):
            f, _ = pos(h)
            multiply(NCH - 1, h, lax.rem(f + 2, RING), place(2 * t + h), TILE)
            far_part(2 * t + h)
        for h in range(2):
            f, _ = pos(h)

            @pl.loop(0, NSTEP - 1)
            def _(i):
                multiply(NCH - 1, h, lax.rem(f + 3 + i, RING), place(2 * t + h), TILE)

    def sent():
        for copy in w_copies:
            copy.wait_send()
        for u in range(UNITS):
            for copy in copies[u]:
                copy.wait_send()

    def sent_part(t, kinds):
        for d in (2 * t, 2 * t + 1):
            for kind in kinds:
                m[d][kind].wait_send()

    near = functools.partial(both, near_part)
    across = functools.partial(both, second)
    finish = functools.partial(both, last)

    steps = {"F": ready, "N": near, "S": across, "L": finish}
    for step, t in ORDER:
        if step == "L" and t == 0:
            sent()
        steps[step](t)
    for t in range(ROWS // 2):
        sent_part(t, range(14))
    for copy in y_copies:
        copy.wait()


def exchange(row_perm, a_cols, b_cols, a_vals, b_vals):
    bf16, f32, i16, i32 = jnp.bfloat16, jnp.float32, jnp.int16, jnp.int32
    t2 = (TILE, TILE)
    b_chunk = pltpu.VMEM((ROWS * PIECE + 1, *t2), bf16)
    dma = pltpu.SemaphoreType.DMA
    return pl.pallas_call(
        kernel,
        out_shape=jax.ShapeDtypeStruct((ROWS, 2, *t2), f32),
        in_specs=[
            pl.BlockSpec(memory_space=pltpu.SMEM),
            pl.BlockSpec(memory_space=pltpu.VMEM),
            pl.BlockSpec(memory_space=pltpu.VMEM),
            pl.BlockSpec(memory_space=pl.ANY),
            pl.BlockSpec(memory_space=pl.ANY),
        ],
        out_specs=pl.BlockSpec(memory_space=pl.ANY),
        scratch_shapes=[
            pltpu.VMEM((ROWS * KA + 1, *t2), bf16),
            b_chunk, b_chunk, b_chunk, b_chunk, b_chunk, b_chunk,
            pltpu.VMEM((ROWS * TILE, CHUNK * TILE), bf16),
            pltpu.VMEM((ROWS * TILE, NC * TILE), f32),
            pltpu.VMEM((ROWS, TILE), i32),
            pltpu.VMEM((ROWS, TILE), i32),
            pltpu.VMEM((NC, TILE), i32),
            pltpu.VMEM((NC, TILE), i32),
            pltpu.VMEM((ROWS, NC, TILE), i32),
            pltpu.SMEM((ROWS, TILE), i32),
            pltpu.SMEM((NC, TILE), i32),
            pltpu.VMEM((ROWS, 2, 4, *t2), i16),
            pltpu.VMEM((ROWS, 2, 8, TILE), f32),
            pltpu.VMEM((ROWS, 2, 4, *t2), i16),
            pltpu.VMEM((ROWS, 2, 8, TILE), f32),
            pltpu.VMEM((ROWS, 2, 8, *t2), i16),
            pltpu.VMEM((ROWS, 2, 8, TILE), f32),
            pltpu.VMEM((ROWS, 2, 8, *t2), i16),
            pltpu.VMEM((ROWS, 2, 8, TILE), f32),
            pltpu.VMEM((ROWS, 3, 2, *t2), i16),
            pltpu.VMEM((ROWS, 3, 8, TILE), f32),
            pltpu.VMEM((ROWS, 3, 2, *t2), i16),
            pltpu.VMEM((ROWS, 3, 8, TILE), f32),
            pltpu.VMEM((ROWS, 2, *t2), f32),
            dma((UNITS, 9)), dma((UNITS, 9)), dma((NCH + 3,)), dma((ROWS,)), dma((ROWS,)),
            dma((ROWS, 14)), dma((ROWS, 14)), dma((ROWS,)), dma((ROWS,)),
        ],
        compiler_params=pltpu.CompilerParams(
            collective_id=0, has_side_effects=True, vmem_limit_bytes=60 * 1024 * 1024
        ),
        name="exchange",
    )(row_perm, a_cols, b_cols, a_vals, b_vals)


def on_device(a_vals, a_cols, b_vals, b_cols, row_perm):
    got = exchange(
        row_perm,
        a_cols.reshape(ROWS, KA),
        b_cols.T,
        a_vals.reshape(ROWS * KA, TILE, TILE),
        b_vals.reshape(KWR * 2, TILE, TILE),
    )
    own_row = lax.axis_index("row")
    source = lax.dynamic_slice_in_dim(row_perm, own_row * ROWS, ROWS) // ROWS
    return got.at[source].get(mode="promise_in_bounds")


def solution(mesh):
    placed = (
        P("row", ("col", "layer"), None, None, None),
        P("row", ("col", "layer"), None),
        P(("col", "layer"), "row", None, None),
        P(("col", "layer"), "row"),
        P(),
    )
    return jax.shard_map(
        on_device,
        mesh=mesh,
        in_specs=placed,
        out_specs=P("row", ("col", "layer"), None, None),
        check_vma=False,
    )
```
